128 devices in a mesh: row: 8 (over x, y_hi), col: 16 (over y_lo, z, core).
Axes of the slice: x: 4, y: 4 (y_hi: 2, y_lo: 2; y = y_hi * 2 + y_lo), z: 4, core: 2. Of those that a mesh axis runs over, the one named last changes fastest.
Arguments:
- amplitudes: float32 [8192, 8192], P('row', 'col'), may hold values from -6 to 6
- integrals: float32 [8192, 8192], P('row', 'col'), may hold values from -12 to 12
- factors: float32 [8192, 1024], P('col'), may hold values from -0.0625 to 0.0625
- pair_order: int32 [8192], replicated, may hold values from 0 to 8191, each once
- occ_energy: float32 [64], replicated, may hold values from -3 to -0.5
- vir_energy: float32 [128], replicated, may hold values from 0.5 to 4
Outputs:
- updated: float32 [8192, 8192], P('row', 'col')
The draws below stay inside these ranges and needn't reach their ends.
Inputs may be any that keep to these rules, and one draw needn't show every extreme that they name: `pair_order`: every pair code appears exactly once.
All inputs are finite; a program needn't handle non-finite values.
Results may differ from the reference program's by a relative error of at most 0.0001.
Values sent between devices are 32-bit elements; how exact they have to be, the bound alone decides.
A program may use at most 64 MiB of HBM per device.

```python
import jax
import jax.numpy as jnp
from jax import lax

NO = 64
NV = 128
KF = 1024
ITERS = 2
P_SIZE = 8192


def block_levels(stream_key, shape, pieces, least, top_value):
    loudness = 1.0
    for axis_at, blocks in pieces:
        draws = jax.random.uniform(jax.random.fold_in(jax.random.fold_in(stream_key, 6), axis_at), (blocks,), jnp.float32, least / len(pieces), top_value / len(pieces))
        loudness = loudness * jnp.repeat(jnp.exp(draws), shape[axis_at] // blocks).reshape((-1,) + (1,) * (len(shape) - 1 - axis_at))
    return loudness


def bell_draw(rng, dims, scale, most, split=(), held_as=jnp.bfloat16):
    array = jax.random.normal(rng, dims, jnp.float32) * scale
    if len(split) > 0:
        array = block_levels(rng, dims, split, -0.22, 0.18) * array
    return jnp.clip(array, min=-most, max=most).astype(held_as)


def setup_inputs(seed: int = 0) -> dict:
    key_list = jax.random.split(jax.random.key(seed), 7)
    return {
        "amplitudes": bell_draw(key_list[0], (P_SIZE, P_SIZE), 1.0, 6.0, ((0, 8), (1, 16)), jnp.float32),
        "integrals": bell_draw(key_list[1], (P_SIZE, P_SIZE), 2.0, 12.0, ((0, 8), (1, 16)), jnp.float32),
        "factors": bell_draw(key_list[2], (P_SIZE, KF), P_SIZE ** -0.5, 0.0625, ((0, 16),), jnp.float32),
        "pair_order": jax.random.permutation(key_list[3], P_SIZE).astype(jnp.int32),
        "occ_energy": jnp.clip(jax.random.uniform(key_list[4], (NO,), jnp.float32, -3.0, -0.5), -3.0, -0.5),
        "vir_energy": jnp.clip(jax.random.uniform(key_list[5], (NV,), jnp.float32, 0.5, 4.0), 0.5, 4.0),
    }


OMEGA = 0.6


def pair_energy(pair_order, occ_energy, vir_energy):
    occupied = pair_order // NV
    virtual = pair_order % NV
    occ_hot = (occupied[:, None] == jnp.arange(NO, dtype=jnp.int32)[None, :]).astype(jnp.float32)
    vir_hot = (virtual[:, None] == jnp.arange(NV, dtype=jnp.int32)[None, :]).astype(jnp.float32)
    high = lax.Precision.HIGHEST
    return jnp.dot(vir_hot, vir_energy, precision=high) - jnp.dot(occ_hot, occ_energy, precision=high)


def contract(left, right):
    return lax.dot_general(left, right, (((1,), (1,)), ((), ())), precision=lax.Precision.HIGHEST)


def reference(amplitudes, integrals, factors, pair_order, occ_energy, vir_energy):
    energy = pair_energy(pair_order, occ_energy, vir_energy)
    denom = energy[:, None] + energy[None, :]
    amp = amplitudes
    for step in range(ITERS):
        inter = jnp.dot(amp, factors, precision=lax.Precision.HIGHEST)
        resid = integrals + contract(inter, factors)
        sym = resid + resid.T
        amp = (1.0 - OMEGA) * amp - OMEGA * sym / denom
    return amp
```

```python
import jax
import jax.numpy as jnp
from jax import lax
from jax.experimental import pallas as pl
from jax.experimental.pallas import tpu as pltpu
from jax.sharding import PartitionSpec as P

NO = 64
NV = 128
OMEGA = 0.6
KEEP = 1.0 - OMEGA

MESH = pl.DeviceIdType.MESH
F32 = jnp.float32
BF16 = jnp.bfloat16
N_SEM = 160


def pair_energy(pair_order, occ_energy, vir_energy):
    occ_hit = (pair_order // NV)[:, None] == jnp.arange(NO, dtype=jnp.int32)[None, :]
    vir_hit = (pair_order % NV)[:, None] == jnp.arange(NV, dtype=jnp.int32)[None, :]
    return jnp.sum(jnp.where(vir_hit, vir_energy[None, :], 0.0), axis=1) - jnp.sum(
        jnp.where(occ_hit, occ_energy[None, :], 0.0), axis=1
    )


def rem(a, b):
    return lax.rem(a, jnp.int32(b))


def div(a, b):
    return lax.div(a, jnp.int32(b))


def split(value):
    high = value.astype(BF16)
    return high, (value - high.astype(F32)).astype(BF16)


def dot_nn(a, b):
    return lax.dot_general(a, b, (((1,), (0,)), ((), ())), preferred_element_type=F32)


def dot_nt(a, b):
    return lax.dot_general(a, b, (((1,), (1,)), ((), ())), preferred_element_type=F32)


def triple(dot, ah, al, bh, bl):
    return dot(ah, bh) + (dot(ah, bl) + dot(al, bh))


class Axis:
    def __init__(self, me, ring, mate, index, device, pick):
        self.me, self.ring, self.mate = me, ring, mate
        self.index, self.device, self.pick = index, device, pick


def kernel(
    a_ref, v_ref, f_ref, er_ref, ec_ref, o_ref,
    a_in, v_in, f_sib, fk_hl, fr, fr_hl, pa, pb, land_c, land_r, mate_c, mate_r,
    sum_c, sum_r, own_c, own_r, inter, y_out, y_in, lh, lf, lt, wr, wk,
    b1, b2, b3, vt_sib, t1, t2, u1, u2, uf, ss, rs, ls,
):
    row = lax.axis_index("row")
    q = lax.axis_index("col")
    c = rem(q, 2)
    o = 1 - c
    k = div(q, 8) * 4 + rem(div(q, 2), 4)
    col_ax = Axis(
        k, rem(div(q, 2), 4), div(q, 8),
        lambda ring, mate: mate * 4 + ring,
        lambda i: (row, div(i, 4) * 8 + rem(i, 4) * 2 + c),
        lambda ref, i: ref.at[i],
    )
    row_ax = Axis(
        row, div(row, 2), rem(row, 2),
        lambda ring, mate: ring * 2 + mate,
        lambda i: (i, q),
        lambda ref, i: ref.at[:, i],
    )
    sibling = (row, q + 1 - 2 * c)

    barrier = pltpu.get_barrier_semaphore()
    for ax in (col_ax, row_ax):
        for d in range(1, 8):
            pl.semaphore_signal(barrier, inc=1, device_id=ax.device(rem(ax.me + d, 8)), device_id_type=MESH)
    pl.semaphore_signal(barrier, inc=1, device_id=sibling, device_id_type=MESH)
    pl.semaphore_wait(barrier, 15)

    used = [0, 0]
    pending = {}

    def send(src, dst, device):
        i = used[0]
        used[0] += 1
        copy = pltpu.make_async_remote_copy(
            src_ref=src, dst_ref=dst, send_sem=ss.at[i], recv_sem=rs.at[i],
            device_id=device, device_id_type=MESH,
        )
        copy.start()
        pending[id(copy)] = copy
        return copy

    def local(src, dst):
        i = used[1]
        used[1] += 1
        copy = pltpu.make_async_copy(src, dst, ls.at[i])
        copy.start()
        return copy

    def sent(copies):
        for copy in copies:
            if pending.pop(id(copy), None) is not None:
                copy.wait_send()

    def all_to_all(ax, src, dst):
        mine = local(src(ax.me), dst(ax.me))
        copies = []
        for d in (4, 3, 5, 2, 6, 1, 7):
            to = rem(ax.me + d, 8)
            copies.append(send(src(to), dst(ax.me), ax.device(to)))

        def wait():
            for copy in copies:
                copy.wait_recv()
            mine.wait()

        return wait

    def scatter_start(ax, part, land):
        copies = []
        for m in range(2):
            mate = (1 - ax.mate) if m == 0 else ax.mate
            for d in (2, 1, 3):
                ring = rem(ax.ring + d, 4)
                copies.append(
                    send(
                        ax.pick(part, ax.index(ring, mate)),
                        land.at[d - 1, m],
                        ax.device(ax.index(ring, ax.mate)),
                    )
                )
        return copies

    def scatter_mate(ax, part, land, copies, stage, mate_land):
        for copy in copies[:3]:
            copy.wait_recv()
        stage[...] = (ax.pick(part, ax.index(ax.ring, 1 - ax.mate))[...] + land[0, 0]) + (land[1, 0] + land[2, 0])
        return send(stage, mate_land, ax.device(ax.index(ax.ring, 1 - ax.mate)))

    def scatter_end(ax, part, land, copies, mate_copy, mate_land):
        for copy in copies[3:]:
            copy.wait_recv()
        value = (ax.pick(part, ax.me)[...] + land[0, 1]) + (land[1, 1] + land[2, 1])
        mate_copy.wait_recv()
        return value + mate_land[...]

    def gather_start(ax, full):
        piece = ax.pick(full, ax.me)
        mate = send(piece, piece, ax.device(ax.index(ax.ring, 1 - ax.mate)))
        copies = []
        for d in (2, 1, 3):
            copies.append(send(piece, piece, ax.device(ax.index(rem(ax.ring + d, 4), ax.mate))))
        return mate, copies

    def gather_forward(ax, full, started):
        mate, copies = started
        mate.wait_recv()
        piece = ax.pick(full, ax.index(ax.ring, 1 - ax.mate))
        for d in (2, 1, 3):
            copies.append(send(piece, piece, ax.device(ax.index(rem(ax.ring + d, 4), ax.mate))))

    def gather_end(started):
        for copy in started[1]:
            copy.wait_recv()

    def lanes(n, size):
        return pl.ds(pl.multiple_of(n * size, size), size)

    a_copy = send(a_ref.at[o], a_in, sibling)
    f_copy = send(f_ref, f_sib, sibling)
    f_hop1 = all_to_all(col_ax, lambda i: f_ref.at[i, row], lambda i: uf.at[i])
    v_copy = send(v_ref.at[o], v_in, sibling)
    v_hop1 = all_to_all(row_ax, lambda i: v_ref.at[:, i], lambda i: b1.at[i])

    fk_hl[0, c], fk_hl[1, c] = split(f_ref[...].reshape(512, 1024))
    lh[0, :, lanes(c, 512)], lh[1, :, lanes(c, 512)] = split(a_ref[c])
    a_copy.wait_recv()
    lh[0, :, lanes(o, 512)], lh[1, :, lanes(o, 512)] = split(a_in[...])
    f_copy.wait_recv()
    fk_hl[0, o], fk_hl[1, o] = split(f_sib[...].reshape(512, 1024))
    f_hop1()
    f_hop2 = all_to_all(row_ax, lambda i: uf.at[i], lambda i: fr.at[c, k, i])

    def product_nn(left, right, out):
        @pl.loop(0, 4)
        def _(n):
            cols = lanes(n, 256)
            res = triple(
                dot_nn, left[0], left[1],
                right[0, :, :, cols].reshape(1024, 256), right[1, :, :, cols].reshape(1024, 256),
            )
            out[:, :, :, cols] = res.reshape(8, 8, 8, 256)

    product_nn(lh, fk_hl, pa)
    rs0 = scatter_start(col_ax, pa, land_c)
    f_hop2()
    f_gather = gather_start(col_ax, fr.at[c])
    mate0 = scatter_mate(col_ax, pa, land_c, rs0, sum_c, mate_c)
    i_own = scatter_end(col_ax, pa, land_c, rs0, mate0, mate_c)
    inter[k] = i_own
    i_gather = gather_start(col_ax, inter)
    gather_forward(col_ax, inter, i_gather)
    gather_forward(col_ax, fr.at[c], f_gather)
    v_hop1()
    v_hop2 = all_to_all(col_ax, lambda i: b1.at[i], lambda i: b2.at[i])
    gather_end(i_gather)

    lf[0], lf[1] = split(inter[...].reshape(512, 1024))
    v_copy.wait_recv()

    @pl.loop(0, 2)
    def _(n):
        rows = lanes(n, 256)
        res = triple(dot_nt, lf[0], lf[1], fk_hl[0, o, rows], fk_hl[1, o, rows])
        drive = v_in[:, :, rows].reshape(512, 256)
        y = (drive + res) / (er_ref[c] + ec_ref[o, :, rows])
        y_out[:, rows] = y
        at = pl.ds(pl.multiple_of(o * 512 + n * 256, 256), 256)
        lh[0, :, at], lh[1, :, at] = split(y)

    y_copy = send(y_out, y_in, sibling)

    @pl.loop(0, 2)
    def _(n):
        rows = lanes(n, 256)
        res = triple(dot_nt, lf[0], lf[1], fk_hl[0, c, rows], fk_hl[1, c, rows])
        drive = v_ref[c, :, :, rows].reshape(512, 256)
        y = (drive + res) / (er_ref[c] + ec_ref[c, :, rows])
        at = pl.ds(pl.multiple_of(c * 512 + n * 256, 256), 256)
        lh[0, :, at], lh[1, :, at] = split(y)
        lt[0, rows, lanes(c, 512)], lt[1, rows, lanes(c, 512)] = split(y.T)

    sent(rs0)
    product_nn(lh, fk_hl, pa)
    rs1_c = scatter_start(col_ax, pa, land_c)
    gather_end(f_gather)
    f_copy2 = send(fr.at[c], fr.at[c], sibling)
    fr_hl[0, c], fr_hl[1, c] = split(fr[c].reshape(512, 1024))
    y_copy.wait_recv()

    @pl.loop(0, 2)
    def _(n):
        rows = lanes(n, 256)
        lt[0, rows, lanes(o, 512)], lt[1, rows, lanes(o, 512)] = split(y_in[:, rows].T)

    f_copy2.wait_recv()
    fr_hl[0, o], fr_hl[1, o] = split(fr[o].reshape(512, 1024))
    product_nn(lt, fr_hl, pb)
    rs1_r = scatter_start(row_ax, pb, land_r)
    v_hop2()
    v_hop3 = all_to_all(row_ax, lambda i: b2.at[i], lambda i: b3.at[i])

    sent([mate0])
    mate1_c = scatter_mate(col_ax, pa, land_c, rs1_c, sum_c, mate_c)
    mate1_r = scatter_mate(row_ax, pb, land_r, rs1_r, sum_r, mate_r)
    own_c[...] = (2.0 * KEEP * OMEGA) * i_own - (OMEGA * OMEGA) * scatter_end(
        col_ax, pa, land_c, rs1_c, mate1_c, mate_c
    )
    c_hop1 = all_to_all(row_ax, lambda i: own_c.at[i], lambda i: t1.at[i])
    own_r[...] = -(OMEGA * OMEGA) * scatter_end(row_ax, pb, land_r, rs1_r, mate1_r, mate_r)
    r_hop1 = all_to_all(col_ax, lambda i: own_r.at[i], lambda i: u1.at[i])
    c_hop1()
    c_hop2 = all_to_all(col_ax, lambda i: t1.at[i], lambda i: t2.at[i])
    r_hop1()
    r_hop2 = all_to_all(row_ax, lambda i: u1.at[i], lambda i: u2.at[i])
    c_hop2()
    row_ax.pick(wk, row)[...] = own_r[...] + t2[...]
    k_gather = gather_start(row_ax, wk)
    r_hop2()
    wr[c, k] = own_c[...] + u2[...]
    r_gather = gather_start(col_ax, wr.at[c])
    gather_forward(row_ax, wk, k_gather)
    gather_forward(col_ax, wr.at[c], r_gather)
    v_hop3()
    vt_copy = send(b3.at[:, o], vt_sib, sibling)
    gather_end(r_gather)
    w_copy = send(wr.at[c], wr.at[c], sibling)
    lf[0], lf[1] = split(wr[c].reshape(512, 1024))
    gather_end(k_gather)
    lt[0], lt[1] = split(wk[...].reshape(512, 1024))

    def finish(half, mirrored):
        @pl.loop(0, 2)
        def _(n):
            rows = lanes(n, 256)
            res = triple(dot_nt, lf[0], lf[1], fk_hl[0, c, rows], fk_hl[1, c, rows])
            res = res + triple(dot_nt, fr_hl[0, half], fr_hl[1, half], lt[0, rows], lt[1, rows])
            drive = v_ref[half, :, :, rows].reshape(512, 256) + mirrored(n).reshape(256, 512).T
            sym = (1.0 + KEEP) * OMEGA * drive + res
            o_ref[half, :, rows] = (KEEP * KEEP) * a_ref[half, :, rows] - sym / (
                er_ref[half] + ec_ref[c, :, rows]
            )

    finish(c, lambda n: b3[pl.ds(n * 4, 4), c])
    w_copy.wait_recv()
    lf[0], lf[1] = split(wr[o].reshape(512, 1024))
    vt_copy.wait_recv()
    finish(o, lambda n: vt_sib[pl.ds(n * 4, 4)])
    sent(list(pending.values()))


def on_device(amplitudes, integrals, factors, pair_order, occ_energy, vir_energy):
    row = lax.axis_index("row")
    q = lax.axis_index("col")
    order = jnp.concatenate(
        [
            lax.dynamic_slice_in_dim(pair_order, row * 1024, 1024, 0),
            lax.dynamic_slice_in_dim(pair_order, (q // 2) * 1024, 1024, 0),
        ]
    )
    energy = pair_energy(order, occ_energy, vir_energy)
    big = lambda *shape: pltpu.VMEM(shape, F32)
    half = lambda *shape: pltpu.VMEM(shape, BF16)
    out = pl.pallas_call(
        kernel,
        out_shape=jax.ShapeDtypeStruct((2, 512, 512), F32),
        in_specs=[pl.BlockSpec(memory_space=pltpu.VMEM)] * 5,
        out_specs=pl.BlockSpec(memory_space=pltpu.VMEM),
        scratch_shapes=[
            big(512, 512),
            big(8, 64, 512),
            big(8, 8, 8, 1024),
            half(2, 2, 512, 1024),
            big(2, 8, 8, 8, 1024),
            half(2, 2, 512, 1024),
            big(8, 8, 8, 1024),
            big(8, 8, 8, 1024),
            big(3, 2, 8, 8, 1024),
            big(3, 2, 8, 8, 1024),
            big(8, 8, 1024),
            big(8, 8, 1024),
            big(8, 8, 1024),
            big(8, 8, 1024),
            big(8, 8, 1024),
            big(8, 8, 1024),
            big(8, 8, 8, 1024),
            big(512, 512),
            big(512, 512),
            half(2, 512, 1024),
            half(2, 512, 1024),
            half(2, 512, 1024),
            big(2, 8, 8, 8, 1024),
            big(8, 8, 8, 1024),
            big(8, 2, 64, 512),
            big(8, 2, 64, 512),
            big(8, 2, 64, 512),
            big(8, 64, 512),
            big(8, 8, 1024),
            big(8, 8, 1024),
            big(8, 8, 1024),
            big(8, 8, 1024),
            big(8, 8, 1024),
            pltpu.SemaphoreType.DMA((N_SEM,)),
            pltpu.SemaphoreType.DMA((N_SEM,)),
            pltpu.SemaphoreType.DMA((16,)),
        ],
        compiler_params=pltpu.CompilerParams(
            collective_id=0, has_side_effects=True, vmem_limit_bytes=63 * 2**20
        ),
        name="lambda_steps",
    )(
        amplitudes.reshape(2, 512, 512),
        integrals.reshape(2, 8, 64, 512),
        factors.reshape(8, 8, 8, 1024),
        energy[:1024].reshape(2, 512, 1),
        energy[1024:].reshape(2, 1, 512),
    )
    return out.reshape(1024, 512)


def solution(mesh):
    return jax.shard_map(
        on_device,
        mesh=mesh,
        in_specs=(P("row", "col"), P("row", "col"), P("col", None), P(), P(), P()),
        out_specs=P("row", "col"),
        check_vma=False,
    )
```

```python
import jax
import jax.numpy as jnp
from jax import lax
from jax.experimental import pallas as pl
from jax.experimental.pallas import tpu as pltpu
from jax.sharding import PartitionSpec as P

NO = 64
NV = 128
OMEGA = 0.6
KEEP = 1.0 - OMEGA

MESH = pl.DeviceIdType.MESH
F32 = jnp.float32
BF16 = jnp.bfloat16
N_SEM = 160


def pair_energy(pair_order, occ_energy, vir_energy):
    occ_hit = (pair_order // NV)[:, None] == jnp.arange(NO, dtype=jnp.int32)[None, :]
    vir_hit = (pair_order % NV)[:, None] == jnp.arange(NV, dtype=jnp.int32)[None, :]
    return jnp.sum(jnp.where(vir_hit, vir_energy[None, :], 0.0), axis=1) - jnp.sum(
        jnp.where(occ_hit, occ_energy[None, :], 0.0), axis=1
    )


def rem(a, b):
    return lax.rem(a, jnp.int32(b))


def div(a, b):
    return lax.div(a, jnp.int32(b))


def split(value):
    high = value.astype(BF16)
    return high, (value - high.astype(F32)).astype(BF16)


def dot_nn(a, b):
    return lax.dot_general(a, b, (((1,), (0,)), ((), ())), preferred_element_type=F32)


def dot_nt(a, b):
    return lax.dot_general(a, b, (((1,), (1,)), ((), ())), preferred_element_type=F32)


def triple(dot, ah, al, bh, bl):
    return dot(ah, bh) + (dot(ah, bl) + dot(al, bh))


class Axis:
    def __init__(self, me, ring, mate, index, device, pick, half):
        self.me, self.ring, self.mate = me, ring, mate
        self.index, self.device, self.pick, self.half = index, device, pick, half


def kernel(
    a_ref, v_ref, f_ref, er_ref, ec_ref, o_ref,
    a_in, v_in, f_sib, fk_hl, fr, fr_hl, pa, pb, far_c, near_c, far_r, near_r, mate_c, mate_r,
    sum_c, sum_r, own_c, own_r, inter, y_out, y_in, lh, lf, lt, wr, wk,
    b1, b2, b3, vt_sib, t1, t2, u1, u2, uf, ss, rs, ls,
):
    row = lax.axis_index("row")
    q = lax.axis_index("col")
    c = rem(q, 2)
    o = 1 - c
    k = div(q, 8) * 4 + rem(div(q, 2), 4)
    col_ax = Axis(
        k, rem(div(q, 2), 4), div(q, 8),
        lambda ring, mate: mate * 4 + ring,
        lambda i: (row, div(i, 4) * 8 + rem(i, 4) * 2 + c),
        lambda ref, i: ref.at[i],
        lambda ref, i, h: ref.at[i, pl.ds(4 * h, 4)],
    )
    row_ax = Axis(
        row, div(row, 2), rem(row, 2),
        lambda ring, mate: ring * 2 + mate,
        lambda i: (i, q),
        lambda ref, i: ref.at[:, i],
        lambda ref, i, h: ref.at[pl.ds(4 * h, 4), i],
    )
    sibling = (row, q + 1 - 2 * c)

    barrier = pltpu.get_barrier_semaphore()
    for ax in (col_ax, row_ax):
        for d in range(1, 8):
            pl.semaphore_signal(barrier, inc=1, device_id=ax.device(rem(ax.me + d, 8)), device_id_type=MESH)
    pl.semaphore_signal(barrier, inc=1, device_id=sibling, device_id_type=MESH)
    pl.semaphore_wait(barrier, 15)

    used = [0, 0]
    pending = {}

    def send(src, dst, device):
        i = used[0]
        used[0] += 1
        copy = pltpu.make_async_remote_copy(
            src_ref=src, dst_ref=dst, send_sem=ss.at[i], recv_sem=rs.at[i],
            device_id=device, device_id_type=MESH,
        )
        copy.start()
        pending[id(copy)] = copy
        return copy

    def local(src, dst):
        i = used[1]
        used[1] += 1
        copy = pltpu.make_async_copy(src, dst, ls.at[i])
        copy.start()
        return copy

    def sent(copies):
        for copy in copies:
            if pending.pop(id(copy), None) is not None:
                copy.wait_send()

    def all_to_all(ax, src, dst):
        mine = local(src(ax.me), dst(ax.me))
        copies = []
        for d in (4, 3, 5, 2, 6, 1, 7):
            to = rem(ax.me + d, 8)
            copies.append(send(src(to), dst(ax.me), ax.device(to)))

        def wait():
            for copy in copies:
                copy.wait_recv()
            mine.wait()

        return wait

    class Scatter:
        def __init__(self, ax, part, far, near, stage, mate_land):
            self.ax, self.part, self.far, self.near = ax, part, far, near
            self.stage, self.mate_land = stage, mate_land
            self.far_copies, self.near_copies = [None, None], [None, None]

        def at(self, d, m):
            mate = (1 - self.ax.mate) if m == 0 else self.ax.mate
            return self.ax.index(rem(self.ax.ring + d, 4), mate)

        def next(self, d):
            return self.ax.device(self.ax.index(rem(self.ax.ring + d, 4), self.ax.mate))

        def start(self, m):
            self.far_copies[m] = [
                send(self.ax.half(self.part, self.at(2, m), h), self.far.at[m, h], self.next((1, 3)[h]))
                for h in range(2)
            ]

        def step(self, m):
            self.near_copies[m] = []
            for h in range(2):
                d = (1, 3)[h]
                self.far_copies[m][h].wait_recv()
                half = self.ax.half(self.part, self.at(d, m), h)
                half[...] = half[...] + self.far[m, h]
                self.near_copies[m].append(
                    send(self.ax.pick(self.part, self.at(d, m)), self.near.at[m, h], self.next(d))
                )

        def total(self, m):
            for copy in self.near_copies[m]:
                copy.wait_recv()
            return self.ax.pick(self.part, self.at(0, m))[...] + (self.near[m, 0] + self.near[m, 1])

        def to_mate(self):
            self.stage[...] = self.total(0)
            self.mate_copy = send(self.stage, self.mate_land, self.ax.device(self.at(0, 0)))

        def end(self):
            value = self.total(1)
            self.mate_copy.wait_recv()
            return value + self.mate_land[...]

        def copies(self):
            return sum(self.far_copies + self.near_copies, []) + [self.mate_copy]

    class Gather:
        def __init__(self, ax, full, also=None):
            self.ax, self.full = ax, full
            self.also = also if also is not None else (lambda ref: None)

        def at(self, d, m):
            mate = (1 - self.ax.mate) if m == 0 else self.ax.mate
            return self.ax.index(rem(self.ax.ring + d, 4), mate)

        def both_ways(self, m):
            piece = self.ax.pick(self.full, self.at(0, m))
            self.also(piece)
            return [send(piece, piece, self.ax.device(self.at(d, 1))) for d in (1, 3)]

        def onward(self, m, copies):
            out = []
            for h in range(2):
                copies[h].wait_recv()
                i = self.at((3, 1)[h], m)
                piece = self.ax.half(self.full, i, h)
                out.append(send(piece, piece, self.ax.device(self.at((1, 3)[h], 1))))
                self.also(self.ax.pick(self.full, i))
            return out

        def start(self):
            piece = self.ax.pick(self.full, self.ax.me)
            self.mate_copy = send(piece, piece, self.ax.device(self.at(0, 0)))
            self.own = self.both_ways(1)

        def step1(self):
            self.own_far = self.onward(1, self.own)

        def step2(self):
            self.mate_copy.wait_recv()
            self.other = self.both_ways(0)

        def step3(self):
            self.other_far = self.onward(0, self.other)

        def end(self):
            for m, copies in ((1, self.own_far), (0, self.other_far)):
                for copy in copies:
                    copy.wait_recv()
                self.also(self.ax.pick(self.full, self.at(2, m)))

    def lanes(n, size):
        return pl.ds(pl.multiple_of(n * size, size), size)

    a_copy = send(a_ref.at[o], a_in, sibling)
    f_copy = send(f_ref, f_sib, sibling)
    f_hop1 = all_to_all(col_ax, lambda i: f_ref.at[i, row], lambda i: uf.at[i])

    fk_hl[0, c], fk_hl[1, c] = split(f_ref[...].reshape(512, 1024))
    lh[0, :, lanes(c, 512)], lh[1, :, lanes(c, 512)] = split(a_ref[c])
    a_copy.wait_recv()
    lh[0, :, lanes(o, 512)], lh[1, :, lanes(o, 512)] = split(a_in[...])
    f_hop1()
    f_hop2 = all_to_all(row_ax, lambda i: uf.at[i], lambda i: fr.at[c, k, i])
    f_copy.wait_recv()
    fk_hl[0, o], fk_hl[1, o] = split(f_sib[...].reshape(512, 1024))

    def product_nn(left, right, out):
        @pl.loop(0, 4)
        def _(n):
            cols = lanes(n, 256)
            res = triple(
                dot_nn, left[0], left[1],
                right[0, :, :, cols].reshape(1024, 256), right[1, :, :, cols].reshape(1024, 256),
            )
            out[:, :, :, cols] = res.reshape(8, 8, 8, 256)

    product_nn(lh, fk_hl, pa)
    rs0 = Scatter(col_ax, pa, far_c, near_c, sum_c, mate_c)
    rs0.start(0)
    rs0.start(1)
    v_copy = send(v_ref.at[o], v_in, sibling)
    f_hop2()
    f_gather = Gather(col_ax, fr.at[c], lambda piece: f_also.append(send(piece, piece, sibling)))
    f_also = []
    f_gather.start()
    rs0.step(0)
    rs0.step(1)
    v_hop1 = all_to_all(row_ax, lambda i: v_ref.at[:, i], lambda i: b1.at[i])
    rs0.to_mate()
    f_gather.step1()
    inter[k] = rs0.end()
    i_gather = Gather(col_ax, inter)
    i_gather.start()
    f_gather.step2()
    i_gather.step1()
    i_gather.step2()
    f_gather.step3()
    i_gather.step3()
    v_hop1()
    i_gather.end()
    v_hop2 = all_to_all(col_ax, lambda i: b1.at[i], lambda i: b2.at[i])

    lf[0], lf[1] = split(inter[...].reshape(512, 1024))
    v_copy.wait_recv()

    @pl.loop(0, 2)
    def _(n):
        rows = lanes(n, 256)
        res = triple(dot_nt, lf[0], lf[1], fk_hl[0, o, rows], fk_hl[1, o, rows])
        drive = v_in[:, :, rows].reshape(512, 256)
        y = (drive + res) / (er_ref[c] + ec_ref[o, :, rows])
        y_out[:, rows] = y
        at = pl.ds(pl.multiple_of(o * 512 + n * 256, 256), 256)
        lh[0, :, at], lh[1, :, at] = split(y)

    y_copy = send(y_out, y_in, sibling)

    @pl.loop(0, 2)
    def _(n):
        rows = lanes(n, 256)
        res = triple(dot_nt, lf[0], lf[1], fk_hl[0, c, rows], fk_hl[1, c, rows])
        drive = v_ref[c, :, :, rows].reshape(512, 256)
        y = (drive + res) / (er_ref[c] + ec_ref[c, :, rows])
        at = pl.ds(pl.multiple_of(c * 512 + n * 256, 256), 256)
        lh[0, :, at], lh[1, :, at] = split(y)
        lt[0, rows, lanes(c, 512)], lt[1, rows, lanes(c, 512)] = split(y.T)

    sent(rs0.copies())
    product_nn(lh, fk_hl, pa)
    rs1_c = Scatter(col_ax, pa, far_c, near_c, sum_c, mate_c)
    rs1_c.start(0)
    rs1_c.start(1)
    f_gather.end()
    fr_hl[0, c], fr_hl[1, c] = split(fr[c].reshape(512, 1024))
    y_copy.wait_recv()

    @pl.loop(0, 2)
    def _(n):
        rows = lanes(n, 256)
        lt[0, rows, lanes(o, 512)], lt[1, rows, lanes(o, 512)] = split(y_in[:, rows].T)

    rs1_c.step(0)
    rs1_c.step(1)
    for copy in f_also:
        copy.wait_recv()
    fr_hl[0, o], fr_hl[1, o] = split(fr[o].reshape(512, 1024))
    product_nn(lt, fr_hl, pb)
    rs1_r = Scatter(row_ax, pb, far_r, near_r, sum_r, mate_r)
    rs1_r.start(0)
    rs1_r.start(1)
    rs1_c.to_mate()
    v_hop2()
    v_hop3 = all_to_all(row_ax, lambda i: b2.at[i], lambda i: b3.at[i])

    rs1_r.step(0)
    rs1_r.step(1)
    own_c[...] = (2.0 * KEEP * OMEGA) * inter[k] - (OMEGA * OMEGA) * rs1_c.end()
    c_hop1 = all_to_all(row_ax, lambda i: own_c.at[i], lambda i: t1.at[i])
    rs1_r.to_mate()
    own_r[...] = -(OMEGA * OMEGA) * rs1_r.end()
    r_hop1 = all_to_all(col_ax, lambda i: own_r.at[i], lambda i: u1.at[i])
    c_hop1()
    c_hop2 = all_to_all(col_ax, lambda i: t1.at[i], lambda i: t2.at[i])
    r_hop1()
    r_hop2 = all_to_all(row_ax, lambda i: u1.at[i], lambda i: u2.at[i])
    c_hop2()
    row_ax.pick(wk, row)[...] = own_r[...] + t2[...]
    k_gather = Gather(row_ax, wk)
    k_gather.start()
    r_hop2()
    wr[c, k] = own_c[...] + u2[...]
    r_gather = Gather(col_ax, wr.at[c])
    r_gather.start()
    k_gather.step1()
    r_gather.step1()
    k_gather.step2()
    r_gather.step2()
    k_gather.step3()
    r_gather.step3()
    v_hop3()
    vt_copy = send(b3.at[:, o], vt_sib, sibling)
    r_gather.end()
    w_copy = send(wr.at[c], wr.at[c], sibling)
    lf[0], lf[1] = split(wr[c].reshape(512, 1024))
    k_gather.end()
    lt[0], lt[1] = split(wk[...].reshape(512, 1024))

    def finish(half, mirrored):
        @pl.loop(0, 2)
        def _(n):
            rows = lanes(n, 256)
            res = triple(dot_nt, lf[0], lf[1], fk_hl[0, c, rows], fk_hl[1, c, rows])
            res = res + triple(dot_nt, fr_hl[0, half], fr_hl[1, half], lt[0, rows], lt[1, rows])
            drive = v_ref[half, :, :, rows].reshape(512, 256) + mirrored(n).reshape(256, 512).T
            sym = (1.0 + KEEP) * OMEGA * drive + res
            o_ref[half, :, rows] = (KEEP * KEEP) * a_ref[half, :, rows] - sym / (
                er_ref[half] + ec_ref[c, :, rows]
            )

    finish(c, lambda n: b3[pl.ds(n * 4, 4), c])
    w_copy.wait_recv()
    lf[0], lf[1] = split(wr[o].reshape(512, 1024))
    vt_copy.wait_recv()
    finish(o, lambda n: vt_sib[pl.ds(n * 4, 4)])
    sent(list(pending.values()))


def on_device(amplitudes, integrals, factors, pair_order, occ_energy, vir_energy):
    row = lax.axis_index("row")
    q = lax.axis_index("col")
    order = jnp.concatenate(
        [
            lax.dynamic_slice_in_dim(pair_order, row * 1024, 1024, 0),
            lax.dynamic_slice_in_dim(pair_order, (q // 2) * 1024, 1024, 0),
        ]
    )
    energy = pair_energy(order, occ_energy, vir_energy)
    big = lambda *shape: pltpu.VMEM(shape, F32)
    half = lambda *shape: pltpu.VMEM(shape, BF16)
    out = pl.pallas_call(
        kernel,
        out_shape=jax.ShapeDtypeStruct((2, 512, 512), F32),
        in_specs=[pl.BlockSpec(memory_space=pltpu.VMEM)] * 5,
        out_specs=pl.BlockSpec(memory_space=pltpu.VMEM),
        scratch_shapes=[
            big(512, 512),
            big(8, 64, 512),
            big(8, 8, 8, 1024),
            half(2, 2, 512, 1024),
            big(2, 8, 8, 8, 1024),
            half(2, 2, 512, 1024),
            big(8, 8, 8, 1024),
            big(8, 8, 8, 1024),
            big(2, 2, 4, 8, 1024),
            big(2, 2, 8, 8, 1024),
            big(2, 2, 4, 8, 1024),
            big(2, 2, 8, 8, 1024),
            big(8, 8, 1024),
            big(8, 8, 1024),
            big(8, 8, 1024),
            big(8, 8, 1024),
            big(8, 8, 1024),
            big(8, 8, 1024),
            big(8, 8, 8, 1024),
            big(512, 512),
            big(512, 512),
            half(2, 512, 1024),
            half(2, 512, 1024),
            half(2, 512, 1024),
            big(2, 8, 8, 8, 1024),
            big(8, 8, 8, 1024),
            big(8, 2, 64, 512),
            big(8, 2, 64, 512),
            big(8, 2, 64, 512),
            big(8, 64, 512),
            big(8, 8, 1024),
            big(8, 8, 1024),
            big(8, 8, 1024),
            big(8, 8, 1024),
            big(8, 8, 1024),
            pltpu.SemaphoreType.DMA((N_SEM,)),
            pltpu.SemaphoreType.DMA((N_SEM,)),
            pltpu.SemaphoreType.DMA((16,)),
        ],
        compiler_params=pltpu.CompilerParams(
            collective_id=0, has_side_effects=True, vmem_limit_bytes=63 * 2**20
        ),
        name="lambda_steps",
    )(
        amplitudes.reshape(2, 512, 512),
        integrals.reshape(2, 8, 64, 512),
        factors.reshape(8, 8, 8, 1024),
        energy[:1024].reshape(2, 512, 1),
        energy[1024:].reshape(2, 1, 512),
    )
    return out.reshape(1024, 512)


def solution(mesh):
    return jax.shard_map(
        on_device,
        mesh=mesh,
        in_specs=(P("row", "col"), P("row", "col"), P("col", None), P(), P(), P()),
        out_specs=P("row", "col"),
        check_vma=False,
    )
```

```python
import jax
import jax.numpy as jnp
from jax import lax
from jax.experimental import pallas as pl
from jax.experimental.pallas import tpu as pltpu
from jax.sharding import PartitionSpec as P

NO = 64
NV = 128
OMEGA = 0.6
KEEP = 1.0 - OMEGA

MESH = pl.DeviceIdType.MESH
F32 = jnp.float32
BF16 = jnp.bfloat16
N_SEM = 160


def pair_energy(pair_order, occ_energy, vir_energy):
    occ_hit = (pair_order // NV)[:, None] == jnp.arange(NO, dtype=jnp.int32)[None, :]
    vir_hit = (pair_order % NV)[:, None] == jnp.arange(NV, dtype=jnp.int32)[None, :]
    return jnp.sum(jnp.where(vir_hit, vir_energy[None, :], 0.0), axis=1) - jnp.sum(
        jnp.where(occ_hit, occ_energy[None, :], 0.0), axis=1
    )


def rem(a, b):
    return lax.rem(a, jnp.int32(b))


def div(a, b):
    return lax.div(a, jnp.int32(b))


def split(value):
    high = value.astype(BF16)
    return high, (value - high.astype(F32)).astype(BF16)


def dot_nn(a, b):
    return lax.dot_general(a, b, (((1,), (0,)), ((), ())), preferred_element_type=F32)


def dot_nt(a, b):
    return lax.dot_general(a, b, (((1,), (1,)), ((), ())), preferred_element_type=F32)


def triple(dot, ah, al, bh, bl):
    return dot(ah, bh) + (dot(ah, bl) + dot(al, bh))


class Axis:
    def __init__(self, me, ring, mate, index, device, pick, half):
        self.me, self.ring, self.mate = me, ring, mate
        self.index, self.device, self.pick, self.half = index, device, pick, half


def kernel(
    a_ref, v_ref, f_ref, er_ref, ec_ref, o_ref,
    a_in, v_in, f_sib, fk_hl, fr, fr_hl, pa, far_c, near_c, far_r, near_r, mate_c, mate_r,
    sum_c, sum_r, own_c, own_r, inter, y_in, lh, lf, lt, wr, wk,
    b1, b2, b3, vt_sib, t1, t2, u1, u2, fg, ss, rs, ls,
):
    pb, y_out = f_sib, a_in
    row = lax.axis_index("row")
    q = lax.axis_index("col")
    c = rem(q, 2)
    o = 1 - c
    k = div(q, 8) * 4 + rem(div(q, 2), 4)
    col_ax = Axis(
        k, rem(div(q, 2), 4), div(q, 8),
        lambda ring, mate: mate * 4 + ring,
        lambda i: (row, div(i, 4) * 8 + rem(i, 4) * 2 + c),
        lambda ref, i: ref.at[i],
        lambda ref, i, h: ref.at[i, pl.ds(4 * h, 4)],
    )
    row_ax = Axis(
        row, div(row, 2), rem(row, 2),
        lambda ring, mate: ring * 2 + mate,
        lambda i: (i, q),
        lambda ref, i: ref.at[:, i],
        lambda ref, i, h: ref.at[pl.ds(4 * h, 4), i],
    )
    sibling = (row, q + 1 - 2 * c)

    barrier = pltpu.get_barrier_semaphore()
    for ax in (col_ax, row_ax):
        for d in range(1, 8):
            pl.semaphore_signal(barrier, inc=1, device_id=ax.device(rem(ax.me + d, 8)), device_id_type=MESH)
    pl.semaphore_signal(barrier, inc=1, device_id=sibling, device_id_type=MESH)
    pl.semaphore_wait(barrier, 15)

    used = [0, 0]
    pending = {}

    def send(src, dst, device):
        i = used[0]
        used[0] += 1
        copy = pltpu.make_async_remote_copy(
            src_ref=src, dst_ref=dst, send_sem=ss.at[i], recv_sem=rs.at[i],
            device_id=device, device_id_type=MESH,
        )
        copy.start()
        pending[id(copy)] = copy
        return copy

    def local(src, dst):
        i = used[1]
        used[1] += 1
        copy = pltpu.make_async_copy(src, dst, ls.at[i])
        copy.start()
        return copy

    def sent(copies):
        for copy in copies:
            if pending.pop(id(copy), None) is not None:
                copy.wait_send()

    def all_to_all(ax, src, dst):
        mine = local(src(ax.me), dst(ax.me))
        copies = []
        for d in (4, 3, 5, 2, 6, 1, 7):
            to = rem(ax.me + d, 8)
            copies.append(send(src(to), dst(ax.me), ax.device(to)))

        def wait():
            for copy in copies:
                copy.wait_recv()
            mine.wait()

        return wait

    class Scatter:
        def __init__(self, ax, part, far, near, stage, mate_land):
            self.ax, self.part, self.far, self.near = ax, part, far, near
            self.stage, self.mate_land = stage, mate_land
            self.far_copies, self.near_copies = [None, None], [None, None]

        def at(self, d, m):
            mate = (1 - self.ax.mate) if m == 0 else self.ax.mate
            return self.ax.index(rem(self.ax.ring + d, 4), mate)

        def next(self, d):
            return self.ax.device(self.ax.index(rem(self.ax.ring + d, 4), self.ax.mate))

        def start(self, m):
            self.far_copies[m] = [
                send(self.ax.half(self.part, self.at(2, m), h), self.far.at[m, h], self.next((1, 3)[h]))
                for h in range(2)
            ]

        def step(self, m):
            self.near_copies[m] = []
            for h in range(2):
                d = (1, 3)[h]
                self.far_copies[m][h].wait_recv()
                half = self.ax.half(self.part, self.at(d, m), h)
                half[...] = half[...] + self.far[m, h]
                self.near_copies[m].append(
                    send(self.ax.pick(self.part, self.at(d, m)), self.near.at[m, h], self.next(d))
                )

        def total(self, m):
            for copy in self.near_copies[m]:
                copy.wait_recv()
            return self.ax.pick(self.part, self.at(0, m))[...] + (self.near[m, 0] + self.near[m, 1])

        def to_mate(self):
            self.stage[...] = self.total(0)
            self.mate_copy = send(self.stage, self.mate_land, self.ax.device(self.at(0, 0)))

        def end(self):
            value = self.total(1)
            self.mate_copy.wait_recv()
            return value + self.mate_land[...]

        def copies(self):
            return sum(self.far_copies + self.near_copies, []) + [self.mate_copy]

    class Gather:
        def __init__(self, ax, full):
            self.ax, self.full = ax, full

        def at(self, d, m):
            mate = (1 - self.ax.mate) if m == 0 else self.ax.mate
            return self.ax.index(rem(self.ax.ring + d, 4), mate)

        def both_ways(self, m):
            piece = self.ax.pick(self.full, self.at(0, m))
            return [send(piece, piece, self.ax.device(self.at(d, 1))) for d in (1, 3)]

        def onward(self, m, copies):
            out = []
            for h in range(2):
                copies[h].wait_recv()
                i = self.at((3, 1)[h], m)
                piece = self.ax.half(self.full, i, h)
                out.append(send(piece, piece, self.ax.device(self.at((1, 3)[h], 1))))
            return out

        def start(self):
            piece = self.ax.pick(self.full, self.ax.me)
            self.mate_copy = send(piece, piece, self.ax.device(self.at(0, 0)))
            self.own = self.both_ways(1)

        def step1(self):
            self.own_far = self.onward(1, self.own)

        def step2(self):
            self.mate_copy.wait_recv()
            self.other = self.both_ways(0)

        def step3(self):
            self.other_far = self.onward(0, self.other)

        def end(self):
            for copy in self.own_far + self.other_far:
                copy.wait_recv()

    def lanes(n, size):
        return pl.ds(pl.multiple_of(n * size, size), size)

    a_copy = send(a_ref.at[o], a_in, sibling)
    f_copy = send(f_ref, f_sib, sibling)
    f_mine = local(f_ref.at[row], fg.at[k])
    f_mine.wait()
    f_gather = Gather(col_ax, fg)
    f_gather.start()
    v_hop1 = all_to_all(row_ax, lambda i: v_ref.at[:, i], lambda i: b1.at[i])

    fk_hl[0, c], fk_hl[1, c] = split(f_ref[...].reshape(512, 1024))
    lh[0, :, lanes(c, 512)], lh[1, :, lanes(c, 512)] = split(a_ref[c])
    a_copy.wait_recv()
    lh[0, :, lanes(o, 512)], lh[1, :, lanes(o, 512)] = split(a_in[...])
    f_copy.wait_recv()
    fk_hl[0, o], fk_hl[1, o] = split(f_sib[...].reshape(512, 1024))
    f_gather.step1()
    f_gather.step2()

    def product_nn(left, right, out):
        @pl.loop(0, 4)
        def _(n):
            cols = lanes(n, 256)
            res = triple(
                dot_nn, left[0], left[1],
                right[0, :, :, cols].reshape(1024, 256), right[1, :, :, cols].reshape(1024, 256),
            )
            out[:, :, :, cols] = res.reshape(8, 8, 8, 256)

    product_nn(lh, fk_hl, pa)
    rs0 = Scatter(col_ax, pa, far_c, near_c, sum_c, mate_c)
    rs0.start(0)
    rs0.start(1)
    v_copy = send(v_ref.at[o], v_in, sibling)
    rs0.step(0)
    rs0.step(1)
    f_gather.step3()
    rs0.to_mate()
    inter[k] = rs0.end()
    i_gather = Gather(col_ax, inter)
    i_gather.start()
    f_gather.end()
    f_hop = all_to_all(row_ax, lambda i: fg.at[i], lambda i: fr.at[c, i])
    i_gather.step1()
    i_gather.step2()
    i_gather.step3()
    v_hop1()
    i_gather.end()
    v_hop2 = all_to_all(col_ax, lambda i: b1.at[i], lambda i: b2.at[i])

    lf[0], lf[1] = split(inter[...].reshape(512, 1024))
    v_copy.wait_recv()

    @pl.loop(0, 2)
    def _(n):
        rows = lanes(n, 256)
        res = triple(dot_nt, lf[0], lf[1], fk_hl[0, o, rows], fk_hl[1, o, rows])
        drive = v_in[:, :, rows].reshape(512, 256)
        y = (drive + res) / (er_ref[c] + ec_ref[o, :, rows])
        y_out[:, rows] = y
        at = pl.ds(pl.multiple_of(o * 512 + n * 256, 256), 256)
        lh[0, :, at], lh[1, :, at] = split(y)

    y_copy = send(y_out, y_in, sibling)

    @pl.loop(0, 2)
    def _(n):
        rows = lanes(n, 256)
        res = triple(dot_nt, lf[0], lf[1], fk_hl[0, c, rows], fk_hl[1, c, rows])
        drive = v_ref[c, :, :, rows].reshape(512, 256)
        y = (drive + res) / (er_ref[c] + ec_ref[c, :, rows])
        at = pl.ds(pl.multiple_of(c * 512 + n * 256, 256), 256)
        lh[0, :, at], lh[1, :, at] = split(y)
        lt[0, rows, lanes(c, 512)], lt[1, rows, lanes(c, 512)] = split(y.T)

    sent(rs0.copies())
    product_nn(lh, fk_hl, pa)
    rs1_c = Scatter(col_ax, pa, far_c, near_c, sum_c, mate_c)
    rs1_c.start(0)
    rs1_c.start(1)
    f_hop()
    f_copy2 = send(fr.at[c], fr.at[c], sibling)
    fr_hl[0, c], fr_hl[1, c] = split(fr[c].reshape(512, 1024))
    y_copy.wait_recv()

    @pl.loop(0, 2)
    def _(n):
        rows = lanes(n, 256)
        lt[0, rows, lanes(o, 512)], lt[1, rows, lanes(o, 512)] = split(y_in[:, rows].T)

    rs1_c.step(0)
    rs1_c.step(1)
    f_copy2.wait_recv()
    fr_hl[0, o], fr_hl[1, o] = split(fr[o].reshape(512, 1024))
    product_nn(lt, fr_hl, pb)
    rs1_r = Scatter(row_ax, pb, far_r, near_r, sum_r, mate_r)
    rs1_r.start(0)
    rs1_r.start(1)
    rs1_c.to_mate()

    rs1_r.step(0)
    rs1_r.step(1)
    v_hop2()
    v_hop3 = all_to_all(row_ax, lambda i: b2.at[i], lambda i: b3.at[i])
    own_c[...] = (2.0 * KEEP * OMEGA) * inter[k] - (OMEGA * OMEGA) * rs1_c.end()
    c_hop1 = all_to_all(row_ax, lambda i: own_c.at[i], lambda i: t1.at[i])
    rs1_r.to_mate()
    own_r[...] = -(OMEGA * OMEGA) * rs1_r.end()
    r_hop1 = all_to_all(col_ax, lambda i: own_r.at[i], lambda i: u1.at[i])
    c_hop1()
    c_hop2 = all_to_all(col_ax, lambda i: t1.at[i], lambda i: t2.at[i])
    r_hop1()
    r_hop2 = all_to_all(row_ax, lambda i: u1.at[i], lambda i: u2.at[i])
    c_hop2()
    row_ax.pick(wk, row)[...] = own_r[...] + t2[...]
    k_gather = Gather(row_ax, wk)
    k_gather.start()
    r_hop2()
    wr[c, k] = own_c[...] + u2[...]
    r_gather = Gather(col_ax, wr.at[c])
    r_gather.start()
    k_gather.step1()
    r_gather.step1()
    k_gather.step2()
    r_gather.step2()
    k_gather.step3()
    r_gather.step3()
    v_hop3()
    vt_copy = send(b3.at[:, o], vt_sib, sibling)
    r_gather.end()
    w_copy = send(wr.at[c], wr.at[c], sibling)
    lf[0], lf[1] = split(wr[c].reshape(512, 1024))
    k_gather.end()
    lt[0], lt[1] = split(wk[...].reshape(512, 1024))

    def finish(half, mirrored):
        @pl.loop(0, 2)
        def _(n):
            rows = lanes(n, 256)
            res = triple(dot_nt, lf[0], lf[1], fk_hl[0, c, rows], fk_hl[1, c, rows])
            res = res + triple(dot_nt, fr_hl[0, half], fr_hl[1, half], lt[0, rows], lt[1, rows])
            drive = v_ref[half, :, :, rows].reshape(512, 256) + mirrored(n).reshape(256, 512).T
            sym = (1.0 + KEEP) * OMEGA * drive + res
            o_ref[half, :, rows] = (KEEP * KEEP) * a_ref[half, :, rows] - sym / (
                er_ref[half] + ec_ref[c, :, rows]
            )

    finish(c, lambda n: b3[pl.ds(n * 4, 4), c])
    w_copy.wait_recv()
    lf[0], lf[1] = split(wr[o].reshape(512, 1024))
    vt_copy.wait_recv()
    finish(o, lambda n: vt_sib[pl.ds(n * 4, 4)])
    sent(list(pending.values()))


def on_device(amplitudes, integrals, factors, pair_order, occ_energy, vir_energy):
    row = lax.axis_index("row")
    q = lax.axis_index("col")
    order = jnp.concatenate(
        [
            lax.dynamic_slice_in_dim(pair_order, row * 1024, 1024, 0),
            lax.dynamic_slice_in_dim(pair_order, (q // 2) * 1024, 1024, 0),
        ]
    )
    energy = pair_energy(order, occ_energy, vir_energy)
    big = lambda *shape: pltpu.VMEM(shape, F32)
    half = lambda *shape: pltpu.VMEM(shape, BF16)
    out = pl.pallas_call(
        kernel,
        out_shape=jax.ShapeDtypeStruct((2, 512, 512), F32),
        in_specs=[pl.BlockSpec(memory_space=pltpu.VMEM)] * 5,
        out_specs=pl.BlockSpec(memory_space=pltpu.VMEM),
        scratch_shapes=[
            big(512, 512),
            big(8, 64, 512),
            big(8, 8, 8, 1024),
            half(2, 2, 512, 1024),
            big(2, 8, 8, 8, 1024),
            half(2, 2, 512, 1024),
            big(8, 8, 8, 1024),
            big(2, 2, 4, 8, 1024),
            big(2, 2, 8, 8, 1024),
            big(2, 2, 4, 8, 1024),
            big(2, 2, 8, 8, 1024),
            big(8, 8, 1024),
            big(8, 8, 1024),
            big(8, 8, 1024),
            big(8, 8, 1024),
            big(8, 8, 1024),
            big(8, 8, 1024),
            big(8, 8, 8, 1024),
            big(512, 512),
            half(2, 512, 1024),
            half(2, 512, 1024),
            half(2, 512, 1024),
            big(2, 8, 8, 8, 1024),
            big(8, 8, 8, 1024),
            big(8, 2, 64, 512),
            big(8, 2, 64, 512),
            big(8, 2, 64, 512),
            big(8, 64, 512),
            big(8, 8, 1024),
            big(8, 8, 1024),
            big(8, 8, 1024),
            big(8, 8, 1024),
            big(8, 8, 8, 1024),
            pltpu.SemaphoreType.DMA((N_SEM,)),
            pltpu.SemaphoreType.DMA((N_SEM,)),
            pltpu.SemaphoreType.DMA((16,)),
        ],
        compiler_params=pltpu.CompilerParams(
            collective_id=0, has_side_effects=True, vmem_limit_bytes=63 * 2**20
        ),
        name="lambda_steps",
    )(
        amplitudes.reshape(2, 512, 512),
        integrals.reshape(2, 8, 64, 512),
        factors.reshape(8, 8, 8, 1024),
        energy[:1024].reshape(2, 512, 1),
        energy[1024:].reshape(2, 1, 512),
    )
    return out.reshape(1024, 512)


def solution(mesh):
    return jax.shard_map(
        on_device,
        mesh=mesh,
        in_specs=(P("row", "col"), P("row", "col"), P("col", None), P(), P(), P()),
        out_specs=P("row", "col"),
        check_vma=False,
    )
```

```python
import jax
import jax.numpy as jnp
from jax import lax
from jax.experimental import pallas as pl
from jax.experimental.pallas import tpu as pltpu
from jax.sharding import PartitionSpec as P

NO = 64
NV = 128
OMEGA = 0.6
KEEP = 1.0 - OMEGA

MESH = pl.DeviceIdType.MESH
F32 = jnp.float32
BF16 = jnp.bfloat16
N_SEM = 232


def pair_energy(codes, occ, vir):
    n = codes.shape[1]
    at_occ = lax.broadcasted_iota(jnp.int32, (NO, n), 0)
    at_vir = lax.broadcasted_iota(jnp.int32, (NV, n), 0)
    occ_hit = at_occ == lax.shift_right_logical(codes, jnp.int32(7))
    vir_hit = at_vir == (codes & (NV - 1))
    return jnp.sum(jnp.where(vir_hit, vir, 0.0), axis=0, keepdims=True) - jnp.sum(
        jnp.where(occ_hit, occ, 0.0), axis=0, keepdims=True
    )


def rem(a, b):
    return lax.rem(a, jnp.int32(b))


def div(a, b):
    return lax.div(a, jnp.int32(b))


def split(value):
    high = value.astype(BF16)
    return high, (value - high.astype(F32)).astype(BF16)


def dot_nn(a, b):
    return lax.dot_general(a, b, (((1,), (0,)), ((), ())), preferred_element_type=F32)


def dot_nt(a, b):
    return lax.dot_general(a, b, (((1,), (1,)), ((), ())), preferred_element_type=F32)


def triple(dot, ah, al, bh, bl):
    return dot(ah, bh) + (dot(ah, bl) + dot(al, bh))


class Axis:
    def __init__(self, me, ring, mate, index, device, pick, half):
        self.me, self.ring, self.mate = me, ring, mate
        self.index, self.device, self.pick, self.half = index, device, pick, half


def kernel(
    a_ref, v_ref, f_ref, order_ref, occ_ref, vir_ref, o_ref,
    a_in, v_in, f_sib, fk_hl, fr, fr_hl, pa, far_c, near_c, far_r, near_r, mate_c, mate_r,
    sum_c, sum_r, own_c, own_r, inter, y_in, lh, lf, lt, wr, wk,
    b1, b2, b3, vt_sib, t1, t2, u1, u2, fg, er_ref, ec_ref, ss, rs, ls, fs,
):
    pb, y_out = f_sib, a_in
    row = lax.axis_index("row")
    q = lax.axis_index("col")
    c = rem(q, 2)
    o = 1 - c
    k = div(q, 8) * 4 + rem(div(q, 2), 4)
    col_ax = Axis(
        k, rem(div(q, 2), 4), div(q, 8),
        lambda ring, mate: mate * 4 + ring,
        lambda i: (row, div(i, 4) * 8 + rem(i, 4) * 2 + c),
        lambda ref, i: ref.at[i],
        lambda ref, i, h: ref.at[i, pl.ds(4 * h, 4)],
    )
    row_ax = Axis(
        row, div(row, 2), rem(row, 2),
        lambda ring, mate: ring * 2 + mate,
        lambda i: (i, q),
        lambda ref, i: ref.at[:, i],
        lambda ref, i, h: ref.at[pl.ds(4 * h, 4), i],
    )
    sibling = (row, q + 1 - 2 * c)

    barrier = pltpu.get_barrier_semaphore()
    for ax in (col_ax, row_ax):
        for d in range(1, 8):
            pl.semaphore_signal(barrier, inc=1, device_id=ax.device(rem(ax.me + d, 8)), device_id_type=MESH)
    pl.semaphore_signal(barrier, inc=1, device_id=sibling, device_id_type=MESH)

    def energies(start):
        return pair_energy(
            order_ref[:, pl.ds(pl.multiple_of(start, 1024), 1024)], occ_ref[...], vir_ref[...]
        )

    row_energy, col_energy = energies(row * 1024), energies(k * 1024)
    for h in range(2):
        mine = row_energy[:, h * 512 : (h + 1) * 512]
        er_ref[h] = jnp.broadcast_to(mine, (128, 512)).T
        ec_ref[h] = col_energy[:, h * 512 : (h + 1) * 512]
    pl.semaphore_wait(barrier, 15)

    used = [0, 0]
    pending = {}

    def send(src, dst, device):
        i = used[0]
        used[0] += 1
        copy = pltpu.make_async_remote_copy(
            src_ref=src, dst_ref=dst, send_sem=ss.at[i], recv_sem=rs.at[i],
            device_id=device, device_id_type=MESH,
        )
        copy.start()
        pending[id(copy)] = copy
        return copy

    def local(src, dst):
        i = used[1]
        used[1] += 1
        copy = pltpu.make_async_copy(src, dst, ls.at[i])
        copy.start()
        return copy

    def sent(copies):
        for copy in copies:
            if pending.pop(id(copy), None) is not None:
                copy.wait_send()

    def all_to_all(ax, src, dst):
        mine = local(src(ax.me), dst(ax.me))
        copies = []
        for d in (4, 3, 5, 2, 6, 1, 7):
            to = rem(ax.me + d, 8)
            copies.append(send(src(to), dst(ax.me), ax.device(to)))

        def wait():
            for copy in copies:
                copy.wait_recv()
            mine.wait()

        return wait

    class Scatter:
        def __init__(self, ax, part, far, near, stage, mate_land):
            self.ax, self.part, self.far, self.near = ax, part, far, near
            self.stage, self.mate_land = stage, mate_land
            self.far_copies, self.near_copies = [None, None], [None, None]

        def at(self, d, m):
            mate = (1 - self.ax.mate) if m == 0 else self.ax.mate
            return self.ax.index(rem(self.ax.ring + d, 4), mate)

        def next(self, d):
            return self.ax.device(self.ax.index(rem(self.ax.ring + d, 4), self.ax.mate))

        def start(self, m):
            self.far_copies[m] = [
                send(self.ax.half(self.part, self.at(2, m), h), self.far.at[m, h], self.next((1, 3)[h]))
                for h in range(2)
            ]

        def step(self, m):
            self.near_copies[m] = []
            for h in range(2):
                d = (1, 3)[h]
                self.far_copies[m][h].wait_recv()
                half = self.ax.half(self.part, self.at(d, m), h)
                half[...] = half[...] + self.far[m, h]
                self.near_copies[m].append(
                    send(self.ax.pick(self.part, self.at(d, m)), self.near.at[m, h], self.next(d))
                )

        def total(self, m):
            for copy in self.near_copies[m]:
                copy.wait_recv()
            return self.ax.pick(self.part, self.at(0, m))[...] + (self.near[m, 0] + self.near[m, 1])

        def to_mate(self):
            self.stage[...] = self.total(0)
            self.mate_copy = send(self.stage, self.mate_land, self.ax.device(self.at(0, 0)))

        def end(self):
            value = self.total(1)
            self.mate_copy.wait_recv()
            return value + self.mate_land[...]

        def copies(self):
            return sum(self.far_copies + self.near_copies, []) + [self.mate_copy]

    class Gather:
        def __init__(self, ax, full, also=None):
            self.ax, self.full = ax, full
            self.also = also if also is not None else (lambda i: None)

        def at(self, d, m):
            mate = (1 - self.ax.mate) if m == 0 else self.ax.mate
            return self.ax.index(rem(self.ax.ring + d, 4), mate)

        def both_ways(self, m):
            piece = self.ax.pick(self.full, self.at(0, m))
            self.also(self.at(0, m))
            return [send(piece, piece, self.ax.device(self.at(d, 1))) for d in (1, 3)]

        def onward(self, m, copies):
            out = []
            for h in range(2):
                copies[h].wait_recv()
                i = self.at((3, 1)[h], m)
                piece = self.ax.half(self.full, i, h)
                out.append(send(piece, piece, self.ax.device(self.at((1, 3)[h], 1))))
                self.also(i)
            return out

        def start(self):
            piece = self.ax.pick(self.full, self.ax.me)
            self.mate_copy = send(piece, piece, self.ax.device(self.at(0, 0)))
            self.own = self.both_ways(1)

        def step1(self):
            self.own_far = self.onward(1, self.own)

        def step2(self):
            self.mate_copy.wait_recv()
            self.other = self.both_ways(0)

        def step3(self):
            self.other_far = self.onward(0, self.other)

        def end(self):
            for m, copies in ((1, self.own_far), (0, self.other_far)):
                for copy in copies:
                    copy.wait_recv()
                self.also(self.at(2, m))

    def lanes(n, size):
        return pl.ds(pl.multiple_of(n * size, size), size)

    a_copy = send(a_ref.at[o], a_in, sibling)
    f_copy = send(f_ref, f_sib, sibling)
    f_mine = local(f_ref.at[row], fg.at[k])
    f_mine.wait()
    moves = []

    def move(i):
        n = used[0]
        used[0] += 1
        far = pltpu.make_async_remote_copy(
            src_ref=fg.at[i], dst_ref=fr.at[c, row], send_sem=ss.at[n], recv_sem=fs.at[row],
            device_id=row_ax.device(i), device_id_type=MESH,
        )
        near = pltpu.make_async_copy(fg.at[i], fr.at[c, row], fs.at[8])
        pl.when(i != row)(far.start)
        pl.when(i == row)(near.start)
        moves.append((i, far, near))

    def moved():
        moves[0][2].wait()
        for j in range(8):
            come = pltpu.make_async_remote_copy(
                src_ref=fg.at[j], dst_ref=fr.at[c, j], send_sem=fs.at[9], recv_sem=fs.at[j],
                device_id=row_ax.device(jnp.int32(j)), device_id_type=MESH,
            )
            pl.when(row != j)(come.wait_recv)

    f_gather = Gather(col_ax, fg, move)
    f_gather.start()
    v_hop1 = all_to_all(row_ax, lambda i: v_ref.at[:, i], lambda i: b1.at[i])

    fk_hl[0, c], fk_hl[1, c] = split(f_ref[...].reshape(512, 1024))
    lh[0, :, lanes(c, 512)], lh[1, :, lanes(c, 512)] = split(a_ref[c])
    a_copy.wait_recv()
    lh[0, :, lanes(o, 512)], lh[1, :, lanes(o, 512)] = split(a_in[...])
    f_copy.wait_recv()
    fk_hl[0, o], fk_hl[1, o] = split(f_sib[...].reshape(512, 1024))
    f_gather.step1()
    f_gather.step2()

    def chunk(ref, h):
        return ref.at[(slice(None),) * (len(ref.shape) - 1) + (pl.ds(h * 512, 512),)]

    def product_nn(left, right, out, h):
        @pl.loop(0, 2)
        def _(n):
            cols = pl.ds(pl.multiple_of(h * 512 + n * 256, 256), 256)
            res = triple(
                dot_nn, left[0], left[1],
                right[0, :, :, cols].reshape(1024, 256), right[1, :, :, cols].reshape(1024, 256),
            )
            out[:, :, :, cols] = res.reshape(8, 8, 8, 256)

    def scatters(ax, part, far, near, stage, mate_land):
        return [
            Scatter(ax, chunk(part, h), far.at[h], near.at[h], stage.at[h], mate_land.at[h]) for h in range(2)
        ]

    rs0 = scatters(col_ax, pa, far_c, near_c, sum_c, mate_c)
    i_gather = [Gather(col_ax, chunk(inter, h)) for h in range(2)]
    for h in range(2):
        product_nn(lh, fk_hl, pa, h)
        rs0[h].start(0)
        rs0[h].start(1)
    f_gather.step3()
    v_copy = send(v_ref.at[o], v_in, sibling)
    for h in range(2):
        rs0[h].step(0)
        rs0[h].step(1)
    f_gather.end()
    for h in range(2):
        rs0[h].to_mate()
        chunk(inter, h)[k] = rs0[h].end()
        i_gather[h].start()
    for h in range(2):
        i_gather[h].step1()
        i_gather[h].step2()
    i_gather[0].step3()
    v_hop1()
    i_gather[0].end()
    lf[0, :, :512], lf[1, :, :512] = split(inter[:, :, :, :512].reshape(512, 512))
    i_gather[1].step3()
    moved()
    f_copy2 = send(fr.at[c], fr.at[c], sibling)
    fr_hl[0, c], fr_hl[1, c] = split(fr[c].reshape(512, 1024))
    i_gather[1].end()
    v_hop2 = all_to_all(col_ax, lambda i: b1.at[i], lambda i: b2.at[i])
    lf[0, :, 512:], lf[1, :, 512:] = split(inter[:, :, :, 512:].reshape(512, 512))

    v_copy.wait_recv()

    @pl.loop(0, 2)
    def _(n):
        rows = lanes(n, 256)
        res = triple(dot_nt, lf[0], lf[1], fk_hl[0, o, rows], fk_hl[1, o, rows])
        drive = v_in[:, :, rows].reshape(512, 256)
        y = (drive + res) / (er_ref[c, :, :1] + ec_ref[o, :, rows])
        y_out[:, rows] = y
        at = pl.ds(pl.multiple_of(o * 512 + n * 256, 256), 256)
        lh[0, :, at], lh[1, :, at] = split(y)

    y_copy = send(y_out, y_in, sibling)

    @pl.loop(0, 2)
    def _(n):
        rows = lanes(n, 256)
        res = triple(dot_nt, lf[0], lf[1], fk_hl[0, c, rows], fk_hl[1, c, rows])
        drive = v_ref[c, :, :, rows].reshape(512, 256)
        y = (drive + res) / (er_ref[c, :, :1] + ec_ref[c, :, rows])
        at = pl.ds(pl.multiple_of(c * 512 + n * 256, 256), 256)
        lh[0, :, at], lh[1, :, at] = split(y)
        lt[0, rows, lanes(c, 512)], lt[1, rows, lanes(c, 512)] = split(y.T)

    sent(rs0[0].copies() + rs0[1].copies())
    rs1_c = scatters(col_ax, pa, far_c, near_c, sum_c, mate_c)
    rs1_r = scatters(row_ax, pb, far_r, near_r, sum_r, mate_r)
    for h in range(2):
        product_nn(lh, fk_hl, pa, h)
        rs1_c[h].start(0)
        rs1_c[h].start(1)
    y_copy.wait_recv()

    @pl.loop(0, 2)
    def _(n):
        rows = lanes(n, 256)
        lt[0, rows, lanes(o, 512)], lt[1, rows, lanes(o, 512)] = split(y_in[:, rows].T)

    f_copy2.wait_recv()
    fr_hl[0, o], fr_hl[1, o] = split(fr[o].reshape(512, 1024))
    for h in range(2):
        product_nn(lt, fr_hl, pb, h)
        rs1_r[h].start(0)
        rs1_r[h].start(1)
        rs1_c[h].step(0)
        rs1_c[h].step(1)

    c_hop1, r_hop1, c_hop2, r_hop2 = [None] * 2, [None] * 2, [None] * 2, [None] * 2
    k_gather = [Gather(row_ax, chunk(wk, h)) for h in range(2)]
    r_gather = [Gather(col_ax, chunk(wr.at[c], h)) for h in range(2)]

    def end_c(h):
        own_c[h] = (2.0 * KEEP * OMEGA) * chunk(inter, h)[k] - (OMEGA * OMEGA) * rs1_c[h].end()
        c_hop1[h] = all_to_all(row_ax, lambda i: own_c.at[h, i], lambda i: t1.at[h, i])

    def end_r(h):
        own_r[h] = -(OMEGA * OMEGA) * rs1_r[h].end()
        r_hop1[h] = all_to_all(col_ax, lambda i: own_r.at[h, i], lambda i: u1.at[h, i])

    def second_hops(h):
        c_hop1[h]()
        c_hop2[h] = all_to_all(col_ax, lambda i: t1.at[h, i], lambda i: t2.at[h, i])
        r_hop1[h]()
        r_hop2[h] = all_to_all(row_ax, lambda i: u1.at[h, i], lambda i: u2.at[h, i])

    def start_gathers(h):
        c_hop2[h]()
        row_ax.pick(chunk(wk, h), row)[...] = own_r[h] + t2[h]
        k_gather[h].start()
        r_hop2[h]()
        col_ax.pick(chunk(wr.at[c], h), k)[...] = own_c[h] + u2[h]
        r_gather[h].start()

    rs1_r[0].step(0)
    rs1_c[0].to_mate()
    rs1_r[0].step(1)
    rs1_c[1].to_mate()
    rs1_r[1].step(0)
    rs1_r[1].step(1)
    end_c(0)
    rs1_r[0].to_mate()
    end_r(0)
    end_c(1)
    rs1_r[1].to_mate()
    v_hop2()
    v_hop3 = all_to_all(row_ax, lambda i: b2.at[i], lambda i: b3.at[i])
    second_hops(0)
    end_r(1)
    start_gathers(0)
    second_hops(1)
    for gather in (k_gather[0], r_gather[0]):
        gather.step1()
        gather.step2()
    start_gathers(1)
    k_gather[0].step3()
    r_gather[0].step3()
    for gather in (k_gather[1], r_gather[1]):
        gather.step1()
        gather.step2()

    def take(h):
        cols = pl.ds(h * 512, 512)
        copy = send(chunk(wr.at[c], h), chunk(wr.at[c], h), sibling)
        lf[0, :, cols], lf[1, :, cols] = split(wr[c, :, :, :, cols].reshape(512, 512))
        lt[0, :, cols], lt[1, :, cols] = split(wk[:, :, :, cols].reshape(512, 512))
        return copy

    def take_sibling(h, copy):
        cols = pl.ds(h * 512, 512)
        copy.wait_recv()
        lh[0, :, cols], lh[1, :, cols] = split(wr[o, :, :, :, cols].reshape(512, 512))

    def terms(half, left, n, h):
        rows, cols = lanes(n, 256), pl.ds(h * 512, 512)
        return triple(
            dot_nt, left[0, :, cols], left[1, :, cols], fk_hl[0, c, rows, cols], fk_hl[1, c, rows, cols]
        ) + triple(
            dot_nt, fr_hl[0, half, :, cols], fr_hl[1, half, :, cols], lt[0, rows, cols], lt[1, rows, cols]
        )

    def first(half, left):
        @pl.loop(0, 2)
        def _(n):
            o_ref[half, :, lanes(n, 256)] = terms(half, left, n, 0)

    k_gather[0].end()
    r_gather[0].end()
    w_copy = take(0)
    k_gather[1].step3()
    r_gather[1].step3()
    first(c, lf)
    take_sibling(0, w_copy)
    first(o, lh)
    v_hop3()
    vt_copy = send(b3.at[:, o], vt_sib, sibling)
    k_gather[1].end()
    r_gather[1].end()
    w_copy = take(1)

    def finish(half, left, mirrored):
        @pl.loop(0, 2)
        def _(n):
            rows = lanes(n, 256)
            res = o_ref[half, :, rows] + terms(half, left, n, 1)
            drive = v_ref[half, :, :, rows].reshape(512, 256) + mirrored(n).reshape(256, 512).T
            sym = (1.0 + KEEP) * OMEGA * drive + res
            o_ref[half, :, rows] = (KEEP * KEEP) * a_ref[half, :, rows] - sym / (
                er_ref[half, :, :1] + ec_ref[c, :, rows]
            )

    finish(c, lf, lambda n: b3[pl.ds(n * 4, 4), c])
    take_sibling(1, w_copy)
    vt_copy.wait_recv()
    finish(o, lh, lambda n: vt_sib[pl.ds(n * 4, 4)])
    sent(list(pending.values()))
    for i, far, _ in moves:
        pl.when(i != row)(far.wait_send)


def on_device(amplitudes, integrals, factors, pair_order, occ_energy, vir_energy):
    big = lambda *shape: pltpu.VMEM(shape, F32)
    half = lambda *shape: pltpu.VMEM(shape, BF16)
    out = pl.pallas_call(
        kernel,
        out_shape=jax.ShapeDtypeStruct((2, 512, 512), F32),
        in_specs=[pl.BlockSpec(memory_space=pltpu.VMEM)] * 6,
        out_specs=pl.BlockSpec(memory_space=pltpu.VMEM),
        scratch_shapes=[
            big(512, 512),
            big(8, 64, 512),
            big(8, 8, 8, 1024),
            half(2, 2, 512, 1024),
            big(2, 8, 8, 8, 1024),
            half(2, 2, 512, 1024),
            big(8, 8, 8, 1024),
            big(2, 2, 2, 4, 8, 512),
            big(2, 2, 2, 8, 8, 512),
            big(2, 2, 2, 4, 8, 512),
            big(2, 2, 2, 8, 8, 512),
            big(2, 8, 8, 512),
            big(2, 8, 8, 512),
            big(2, 8, 8, 512),
            big(2, 8, 8, 512),
            big(2, 8, 8, 512),
            big(2, 8, 8, 512),
            big(8, 8, 8, 1024),
            big(512, 512),
            half(2, 512, 1024),
            half(2, 512, 1024),
            half(2, 512, 1024),
            big(2, 8, 8, 8, 1024),
            big(8, 8, 8, 1024),
            big(8, 2, 64, 512),
            big(8, 2, 64, 512),
            big(8, 2, 64, 512),
            big(8, 64, 512),
            big(2, 8, 8, 512),
            big(2, 8, 8, 512),
            big(2, 8, 8, 512),
            big(2, 8, 8, 512),
            big(8, 8, 8, 1024),
            big(2, 512, 128),
            big(2, 1, 512),
            pltpu.SemaphoreType.DMA((N_SEM,)),
            pltpu.SemaphoreType.DMA((N_SEM,)),
            pltpu.SemaphoreType.DMA((16,)),
            pltpu.SemaphoreType.DMA((10,)),
        ],
        compiler_params=pltpu.CompilerParams(
            collective_id=0, has_side_effects=True, vmem_limit_bytes=63 * 2**20
        ),
        name="lambda_steps",
    )(
        amplitudes.reshape(2, 512, 512),
        integrals.reshape(2, 8, 64, 512),
        factors.reshape(8, 8, 8, 1024),
        pair_order.reshape(1, NO * NV),
        occ_energy.reshape(NO, 1),
        vir_energy.reshape(NV, 1),
    )
    return out.reshape(1024, 512)


def solution(mesh):
    return jax.shard_map(
        on_device,
        mesh=mesh,
        in_specs=(P("row", "col"), P("row", "col"), P("col", None), P(), P(), P()),
        out_specs=P("row", "col"),
        check_vma=False,
    )
```

```python
import jax
import jax.numpy as jnp
from jax import lax
from jax.experimental import pallas as pl
from jax.experimental.pallas import tpu as pltpu
from jax.sharding import PartitionSpec as P

NO = 64
NV = 128
OMEGA = 0.6
KEEP = 1.0 - OMEGA

MESH = pl.DeviceIdType.MESH
F32 = jnp.float32
BF16 = jnp.bfloat16
N_SEM = 232


def pair_energy(codes, occ, vir):
    n = codes.shape[1]
    at_occ = lax.broadcasted_iota(jnp.int32, (NO, n), 0)
    at_vir = lax.broadcasted_iota(jnp.int32, (NV, n), 0)
    occ_hit = at_occ == lax.shift_right_logical(codes, jnp.int32(7))
    vir_hit = at_vir == (codes & (NV - 1))
    return jnp.sum(jnp.where(vir_hit, vir, 0.0), axis=0, keepdims=True) - jnp.sum(
        jnp.where(occ_hit, occ, 0.0), axis=0, keepdims=True
    )


def rem(a, b):
    return lax.rem(a, jnp.int32(b))


def div(a, b):
    return lax.div(a, jnp.int32(b))


def split(value):
    high = value.astype(BF16)
    return high, (value - high.astype(F32)).astype(BF16)


def dot_nn(a, b):
    return lax.dot_general(a, b, (((1,), (0,)), ((), ())), preferred_element_type=F32)


def dot_nt(a, b):
    return lax.dot_general(a, b, (((1,), (1,)), ((), ())), preferred_element_type=F32)


def triple(dot, ah, al, bh, bl):
    return dot(ah, bh) + (dot(ah, bl) + dot(al, bh))


class Axis:
    def __init__(self, me, ring, mate, index, device, pick, half):
        self.me, self.ring, self.mate = me, ring, mate
        self.index, self.device, self.pick, self.half = index, device, pick, half


def kernel(
    a_ref, v_ref, f_ref, order_ref, occ_ref, vir_ref, o_ref,
    a_in, v_in, f_sib, fk_hl, fr, fr_hl, pa, far_c, near_c, far_r, near_r, mate_c, mate_r,
    sum_c, sum_r, own_c, own_r, inter, y_in, lh, lf, lt, wr, wk,
    b1, b2, b3, vt_sib, t1, t2, u1, u2, fg, er_ref, ec_ref, ss, rs, ls,
):
    pb, y_out = f_sib, a_in
    row = lax.axis_index("row")
    q = lax.axis_index("col")
    c = rem(q, 2)
    o = 1 - c
    k = div(q, 8) * 4 + rem(div(q, 2), 4)
    col_ax = Axis(
        k, rem(div(q, 2), 4), div(q, 8),
        lambda ring, mate: mate * 4 + ring,
        lambda i: (row, div(i, 4) * 8 + rem(i, 4) * 2 + c),
        lambda ref, i: ref.at[i],
        lambda ref, i, h: ref.at[i, pl.ds(4 * h, 4)],
    )
    row_ax = Axis(
        row, div(row, 2), rem(row, 2),
        lambda ring, mate: ring * 2 + mate,
        lambda i: (i, q),
        lambda ref, i: ref.at[:, i],
        lambda ref, i, h: ref.at[pl.ds(4 * h, 4), i],
    )
    sibling = (row, q + 1 - 2 * c)

    barrier = pltpu.get_barrier_semaphore()
    for ax in (col_ax, row_ax):
        for d in range(1, 8):
            pl.semaphore_signal(barrier, inc=1, device_id=ax.device(rem(ax.me + d, 8)), device_id_type=MESH)
    pl.semaphore_signal(barrier, inc=1, device_id=sibling, device_id_type=MESH)

    def energies(start):
        return pair_energy(
            order_ref[:, pl.ds(pl.multiple_of(start, 1024), 1024)], occ_ref[...], vir_ref[...]
        )

    row_energy, col_energy = energies(row * 1024), energies(k * 1024)
    for h in range(2):
        mine = row_energy[:, h * 512 : (h + 1) * 512]
        er_ref[h] = jnp.broadcast_to(mine, (128, 512)).T
        ec_ref[h] = col_energy[:, h * 512 : (h + 1) * 512]
    pl.semaphore_wait(barrier, 15)

    used = [0, 0]
    pending = {}

    def send(src, dst, device):
        i = used[0]
        used[0] += 1
        copy = pltpu.make_async_remote_copy(
            src_ref=src, dst_ref=dst, send_sem=ss.at[i], recv_sem=rs.at[i],
            device_id=device, device_id_type=MESH,
        )
        copy.start()
        pending[id(copy)] = copy
        return copy

    def local(src, dst):
        i = used[1]
        used[1] += 1
        copy = pltpu.make_async_copy(src, dst, ls.at[i])
        copy.start()
        return copy

    def sent(copies):
        for copy in copies:
            if pending.pop(id(copy), None) is not None:
                copy.wait_send()

    def all_to_all(ax, src, dst):
        mine = local(src(ax.me), dst(ax.me))
        copies = []
        for d in (4, 3, 5, 2, 6, 1, 7):
            to = rem(ax.me + d, 8)
            copies.append(send(src(to), dst(ax.me), ax.device(to)))

        def wait():
            for copy in copies:
                copy.wait_recv()
            mine.wait()

        return wait

    class Scatter:
        def __init__(self, ax, part, far, near, stage, mate_land):
            self.ax, self.part, self.far, self.near = ax, part, far, near
            self.stage, self.mate_land = stage, mate_land
            self.far_copies, self.near_copies = [None, None], [None, None]

        def at(self, d, m):
            mate = (1 - self.ax.mate) if m == 0 else self.ax.mate
            return self.ax.index(rem(self.ax.ring + d, 4), mate)

        def next(self, d):
            return self.ax.device(self.ax.index(rem(self.ax.ring + d, 4), self.ax.mate))

        def start(self, m):
            self.far_copies[m] = [
                send(self.ax.half(self.part, self.at(2, m), h), self.far.at[m, h], self.next((1, 3)[h]))
                for h in range(2)
            ]

        def step(self, m):
            self.near_copies[m] = []
            for h in range(2):
                d = (1, 3)[h]
                self.far_copies[m][h].wait_recv()
                half = self.ax.half(self.part, self.at(d, m), h)
                half[...] = half[...] + self.far[m, h]
                self.near_copies[m].append(
                    send(self.ax.pick(self.part, self.at(d, m)), self.near.at[m, h], self.next(d))
                )

        def total(self, m):
            for copy in self.near_copies[m]:
                copy.wait_recv()
            return self.ax.pick(self.part, self.at(0, m))[...] + (self.near[m, 0] + self.near[m, 1])

        def to_mate(self):
            self.stage[...] = self.total(0)
            self.mate_copy = send(self.stage, self.mate_land, self.ax.device(self.at(0, 0)))

        def end(self):
            value = self.total(1)
            self.mate_copy.wait_recv()
            return value + self.mate_land[...]

        def copies(self):
            return sum(self.far_copies + self.near_copies, []) + [self.mate_copy]

    class Gather:
        def __init__(self, ax, full, also=None):
            self.ax, self.full = ax, full
            self.also = also if also is not None else (lambda i: None)

        def at(self, d, m):
            mate = (1 - self.ax.mate) if m == 0 else self.ax.mate
            return self.ax.index(rem(self.ax.ring + d, 4), mate)

        def both_ways(self, m):
            piece = self.ax.pick(self.full, self.at(0, m))
            self.also(self.at(0, m))
            return [send(piece, piece, self.ax.device(self.at(d, 1))) for d in (1, 3)]

        def onward(self, m, copies):
            out = []
            for h in range(2):
                copies[h].wait_recv()
                i = self.at((3, 1)[h], m)
                piece = self.ax.half(self.full, i, h)
                out.append(send(piece, piece, self.ax.device(self.at((1, 3)[h], 1))))
                self.also(i)
            return out

        def start(self):
            piece = self.ax.pick(self.full, self.ax.me)
            self.mate_copy = send(piece, piece, self.ax.device(self.at(0, 0)))
            self.own = self.both_ways(1)

        def step1(self):
            self.own_far = self.onward(1, self.own)

        def step2(self):
            self.mate_copy.wait_recv()
            self.other = self.both_ways(0)

        def step3(self):
            self.other_far = self.onward(0, self.other)

        def end(self):
            for m, copies in ((1, self.own_far), (0, self.other_far)):
                for copy in copies:
                    copy.wait_recv()
                self.also(self.at(2, m))

    def lanes(n, size):
        return pl.ds(pl.multiple_of(n * size, size), size)

    a_copy = send(a_ref.at[o], a_in, sibling)
    f_copy = send(f_ref, f_sib, sibling)
    f_mine = local(f_ref.at[row], fg.at[k])
    f_mine.wait()
    f_gather = Gather(col_ax, fg)
    f_gather.start()
    v_hop1 = all_to_all(row_ax, lambda i: v_ref.at[:, i], lambda i: b1.at[i])

    fk_hl[0, c], fk_hl[1, c] = split(f_ref[...].reshape(512, 1024))
    lh[0, :, lanes(c, 512)], lh[1, :, lanes(c, 512)] = split(a_ref[c])
    a_copy.wait_recv()
    lh[0, :, lanes(o, 512)], lh[1, :, lanes(o, 512)] = split(a_in[...])
    f_copy.wait_recv()
    fk_hl[0, o], fk_hl[1, o] = split(f_sib[...].reshape(512, 1024))
    f_gather.step1()
    f_gather.step2()

    def chunk(ref, h):
        return ref.at[(slice(None),) * (len(ref.shape) - 1) + (pl.ds(h * 512, 512),)]

    def product_nn(left, right, out, h):
        @pl.loop(0, 2)
        def _(n):
            cols = pl.ds(pl.multiple_of(h * 512 + n * 256, 256), 256)
            res = triple(
                dot_nn, left[0], left[1],
                right[0, :, :, cols].reshape(1024, 256), right[1, :, :, cols].reshape(1024, 256),
            )
            out[:, :, :, cols] = res.reshape(8, 8, 8, 256)

    def scatters(ax, part, far, near, stage, mate_land):
        return [
            Scatter(ax, chunk(part, h), far.at[h], near.at[h], stage.at[h], mate_land.at[h]) for h in range(2)
        ]

    rs0 = scatters(col_ax, pa, far_c, near_c, sum_c, mate_c)
    i_gather = [Gather(col_ax, chunk(inter, h)) for h in range(2)]
    for h in range(2):
        product_nn(lh, fk_hl, pa, h)
        rs0[h].start(0)
        rs0[h].start(1)
    f_gather.step3()
    v_copy = send(v_ref.at[o], v_in, sibling)
    rs0[0].step(0)
    rs0[0].step(1)
    rs0[0].to_mate()
    rs0[1].step(0)
    f_gather.end()

    def start_inter(h):
        chunk(inter, h)[k] = rs0[h].end()
        i_gather[h].start()

    start_inter(0)
    rs0[1].step(1)
    rs0[1].to_mate()
    i_gather[0].step1()
    i_gather[0].step2()
    start_inter(1)
    f_hop = all_to_all(row_ax, lambda i: fg.at[i], lambda i: fr.at[c, i])
    i_gather[0].step3()
    i_gather[1].step1()
    i_gather[1].step2()
    i_gather[0].end()
    lf[0, :, :512], lf[1, :, :512] = split(inter[:, :, :, :512].reshape(512, 512))
    i_gather[1].step3()
    i_gather[1].end()
    lf[0, :, 512:], lf[1, :, 512:] = split(inter[:, :, :, 512:].reshape(512, 512))
    v_hop1()
    v_hop2 = all_to_all(col_ax, lambda i: b1.at[i], lambda i: b2.at[i])

    v_copy.wait_recv()

    @pl.loop(0, 2)
    def _(n):
        rows = lanes(n, 256)
        res = triple(dot_nt, lf[0], lf[1], fk_hl[0, o, rows], fk_hl[1, o, rows])
        drive = v_in[:, :, rows].reshape(512, 256)
        y = (drive + res) / (er_ref[c, :, :1] + ec_ref[o, :, rows])
        y_out[:, rows] = y
        at = pl.ds(pl.multiple_of(o * 512 + n * 256, 256), 256)
        lh[0, :, at], lh[1, :, at] = split(y)

    y_copy = send(y_out, y_in, sibling)

    @pl.loop(0, 2)
    def _(n):
        rows = lanes(n, 256)
        res = triple(dot_nt, lf[0], lf[1], fk_hl[0, c, rows], fk_hl[1, c, rows])
        drive = v_ref[c, :, :, rows].reshape(512, 256)
        y = (drive + res) / (er_ref[c, :, :1] + ec_ref[c, :, rows])
        at = pl.ds(pl.multiple_of(c * 512 + n * 256, 256), 256)
        lh[0, :, at], lh[1, :, at] = split(y)
        lt[0, rows, lanes(c, 512)], lt[1, rows, lanes(c, 512)] = split(y.T)

    sent(rs0[0].copies() + rs0[1].copies())
    rs1_c = scatters(col_ax, pa, far_c, near_c, sum_c, mate_c)
    rs1_r = scatters(row_ax, pb, far_r, near_r, sum_r, mate_r)
    for h in range(2):
        product_nn(lh, fk_hl, pa, h)
        rs1_c[h].start(0)
        rs1_c[h].start(1)
    f_hop()
    f_copy2 = send(fr.at[c], fr.at[c], sibling)
    fr_hl[0, c], fr_hl[1, c] = split(fr[c].reshape(512, 1024))
    y_copy.wait_recv()

    @pl.loop(0, 2)
    def _(n):
        rows = lanes(n, 256)
        lt[0, rows, lanes(o, 512)], lt[1, rows, lanes(o, 512)] = split(y_in[:, rows].T)

    f_copy2.wait_recv()
    fr_hl[0, o], fr_hl[1, o] = split(fr[o].reshape(512, 1024))
    for h in range(2):
        product_nn(lt, fr_hl, pb, h)
        rs1_r[h].start(0)
        rs1_r[h].start(1)
        if h == 0:
            rs1_c[0].step(0)
            rs1_c[0].step(1)

    c_hop1, r_hop1, c_hop2, r_hop2 = [None] * 2, [None] * 2, [None] * 2, [None] * 2
    k_gather = [Gather(row_ax, chunk(wk, h)) for h in range(2)]
    r_gather = [Gather(col_ax, chunk(wr.at[c], h)) for h in range(2)]

    def end_c(h):
        own_c[h] = (2.0 * KEEP * OMEGA) * chunk(inter, h)[k] - (OMEGA * OMEGA) * rs1_c[h].end()
        c_hop1[h] = all_to_all(row_ax, lambda i: own_c.at[h, i], lambda i: t1.at[h, i])

    def end_r(h):
        own_r[h] = -(OMEGA * OMEGA) * rs1_r[h].end()
        r_hop1[h] = all_to_all(col_ax, lambda i: own_r.at[h, i], lambda i: u1.at[h, i])

    def second_hops(h):
        c_hop1[h]()
        c_hop2[h] = all_to_all(col_ax, lambda i: t1.at[h, i], lambda i: t2.at[h, i])
        r_hop1[h]()
        r_hop2[h] = all_to_all(row_ax, lambda i: u1.at[h, i], lambda i: u2.at[h, i])

    def start_gathers(h):
        c_hop2[h]()
        row_ax.pick(chunk(wk, h), row)[...] = own_r[h] + t2[h]
        k_gather[h].start()
        r_hop2[h]()
        col_ax.pick(chunk(wr.at[c], h), k)[...] = own_c[h] + u2[h]
        r_gather[h].start()

    rs1_c[0].to_mate()
    rs1_c[1].step(0)
    rs1_r[0].step(0)
    rs1_r[0].step(1)
    end_c(0)
    rs1_c[1].step(1)
    rs1_r[0].to_mate()
    rs1_r[1].step(0)
    rs1_c[1].to_mate()
    end_r(0)
    rs1_r[1].step(1)
    end_c(1)
    rs1_r[1].to_mate()
    v_hop2()
    v_hop3 = all_to_all(row_ax, lambda i: b2.at[i], lambda i: b3.at[i])
    second_hops(0)
    end_r(1)
    start_gathers(0)
    second_hops(1)
    for gather in (k_gather[0], r_gather[0]):
        gather.step1()
        gather.step2()
    start_gathers(1)
    k_gather[0].step3()
    r_gather[0].step3()
    for gather in (k_gather[1], r_gather[1]):
        gather.step1()
        gather.step2()

    def take(h):
        cols = pl.ds(h * 512, 512)
        copy = send(chunk(wr.at[c], h), chunk(wr.at[c], h), sibling)
        lf[0, :, cols], lf[1, :, cols] = split(wr[c, :, :, :, cols].reshape(512, 512))
        lt[0, :, cols], lt[1, :, cols] = split(wk[:, :, :, cols].reshape(512, 512))
        return copy

    def take_sibling(h, copy):
        cols = pl.ds(h * 512, 512)
        copy.wait_recv()
        lh[0, :, cols], lh[1, :, cols] = split(wr[o, :, :, :, cols].reshape(512, 512))

    def terms(half, left, n, h):
        rows, cols = lanes(n, 256), pl.ds(h * 512, 512)
        return triple(
            dot_nt, left[0, :, cols], left[1, :, cols], fk_hl[0, c, rows, cols], fk_hl[1, c, rows, cols]
        ) + triple(
            dot_nt, fr_hl[0, half, :, cols], fr_hl[1, half, :, cols], lt[0, rows, cols], lt[1, rows, cols]
        )

    def first(half, left):
        @pl.loop(0, 2)
        def _(n):
            o_ref[half, :, lanes(n, 256)] = terms(half, left, n, 0)

    k_gather[0].end()
    r_gather[0].end()
    w_copy = take(0)
    k_gather[1].step3()
    r_gather[1].step3()
    first(c, lf)
    take_sibling(0, w_copy)
    first(o, lh)
    v_hop3()
    vt_copy = send(b3.at[:, o], vt_sib, sibling)
    k_gather[1].end()
    r_gather[1].end()
    w_copy = take(1)

    def finish(half, left, mirrored):
        @pl.loop(0, 2)
        def _(n):
            rows = lanes(n, 256)
            res = o_ref[half, :, rows] + terms(half, left, n, 1)
            drive = v_ref[half, :, :, rows].reshape(512, 256) + mirrored(n).reshape(256, 512).T
            sym = (1.0 + KEEP) * OMEGA * drive + res
            o_ref[half, :, rows] = (KEEP * KEEP) * a_ref[half, :, rows] - sym / (
                er_ref[half, :, :1] + ec_ref[c, :, rows]
            )

    finish(c, lf, lambda n: b3[pl.ds(n * 4, 4), c])
    take_sibling(1, w_copy)
    vt_copy.wait_recv()
    finish(o, lh, lambda n: vt_sib[pl.ds(n * 4, 4)])
    sent(list(pending.values()))


def on_device(amplitudes, integrals, factors, pair_order, occ_energy, vir_energy):
    big = lambda *shape: pltpu.VMEM(shape, F32)
    half = lambda *shape: pltpu.VMEM(shape, BF16)
    out = pl.pallas_call(
        kernel,
        out_shape=jax.ShapeDtypeStruct((2, 512, 512), F32),
        in_specs=[pl.BlockSpec(memory_space=pltpu.VMEM)] * 6,
        out_specs=pl.BlockSpec(memory_space=pltpu.VMEM),
        scratch_shapes=[
            big(512, 512),
            big(8, 64, 512),
            big(8, 8, 8, 1024),
            half(2, 2, 512, 1024),
            big(2, 8, 8, 8, 1024),
            half(2, 2, 512, 1024),
            big(8, 8, 8, 1024),
            big(2, 2, 2, 4, 8, 512),
            big(2, 2, 2, 8, 8, 512),
            big(2, 2, 2, 4, 8, 512),
            big(2, 2, 2, 8, 8, 512),
            big(2, 8, 8, 512),
            big(2, 8, 8, 512),
            big(2, 8, 8, 512),
            big(2, 8, 8, 512),
            big(2, 8, 8, 512),
            big(2, 8, 8, 512),
            big(8, 8, 8, 1024),
            big(512, 512),
            half(2, 512, 1024),
            half(2, 512, 1024),
            half(2, 512, 1024),
            big(2, 8, 8, 8, 1024),
            big(8, 8, 8, 1024),
            big(8, 2, 64, 512),
            big(8, 2, 64, 512),
            big(8, 2, 64, 512),
            big(8, 64, 512),
            big(2, 8, 8, 512),
            big(2, 8, 8, 512),
            big(2, 8, 8, 512),
            big(2, 8, 8, 512),
            big(8, 8, 8, 1024),
            big(2, 512, 128),
            big(2, 1, 512),
            pltpu.SemaphoreType.DMA((N_SEM,)),
            pltpu.SemaphoreType.DMA((N_SEM,)),
            pltpu.SemaphoreType.DMA((16,)),
        ],
        compiler_params=pltpu.CompilerParams(
            collective_id=0, has_side_effects=True, vmem_limit_bytes=63 * 2**20
        ),
        name="lambda_steps",
    )(
        amplitudes.reshape(2, 512, 512),
        integrals.reshape(2, 8, 64, 512),
        factors.reshape(8, 8, 8, 1024),
        pair_order.reshape(1, NO * NV),
        occ_energy.reshape(NO, 1),
        vir_energy.reshape(NV, 1),
    )
    return out.reshape(1024, 512)


def solution(mesh):
    return jax.shard_map(
        on_device,
        mesh=mesh,
        in_specs=(P("row", "col"), P("row", "col"), P("col", None), P(), P(), P()),
        out_specs=P("row", "col"),
        check_vma=False,
    )
```

```python
import jax
import jax.numpy as jnp
from jax import lax
from jax.experimental import pallas as pl
from jax.experimental.pallas import tpu as pltpu
from jax.sharding import PartitionSpec as P

NO = 64
NV = 128
OMEGA = 0.6
KEEP = 1.0 - OMEGA

MESH = pl.DeviceIdType.MESH
F32 = jnp.float32
BF16 = jnp.bfloat16
N_SEM = 232


def pair_energy(codes, occ, vir):
    n = codes.shape[1]
    at_occ = lax.broadcasted_iota(jnp.int32, (NO, n), 0)
    at_vir = lax.broadcasted_iota(jnp.int32, (NV, n), 0)
    occ_hit = at_occ == lax.shift_right_logical(codes, jnp.int32(7))
    vir_hit = at_vir == (codes & (NV - 1))
    return jnp.sum(jnp.where(vir_hit, vir, 0.0), axis=0, keepdims=True) - jnp.sum(
        jnp.where(occ_hit, occ, 0.0), axis=0, keepdims=True
    )


def rem(a, b):
    return lax.rem(a, jnp.int32(b))


def div(a, b):
    return lax.div(a, jnp.int32(b))


def split(value):
    high = value.astype(BF16)
    return high, (value - high.astype(F32)).astype(BF16)


def dot_nn(a, b):
    return lax.dot_general(a, b, (((1,), (0,)), ((), ())), preferred_element_type=F32)


def dot_nt(a, b):
    return lax.dot_general(a, b, (((1,), (1,)), ((), ())), preferred_element_type=F32)


def triple(dot, ah, al, bh, bl):
    return dot(ah, bh) + (dot(ah, bl) + dot(al, bh))


class Axis:
    def __init__(self, me, ring, mate, index, device, pick, half):
        self.me, self.ring, self.mate = me, ring, mate
        self.index, self.device, self.pick, self.half = index, device, pick, half


def kernel(
    a_ref, v_ref, f_ref, order_ref, occ_ref, vir_ref, o_ref,
    a_in, v_in, f_sib, fk_hl, fr, fr_hl, pa, far_c, near_c, far_r, near_r, mate_c, mate_r,
    sum_c, sum_r, own_c, own_r, inter, y_in, lh, lf, lt, wr, wk,
    b1, b2, b3, vt_sib, t1, t2, u1, u2, fg, er_ref, ec_ref, ss, rs, ls,
):
    pb, y_out = f_sib, a_in
    row = lax.axis_index("row")
    q = lax.axis_index("col")
    c = rem(q, 2)
    o = 1 - c
    k = div(q, 8) * 4 + rem(div(q, 2), 4)
    col_ax = Axis(
        k, rem(div(q, 2), 4), div(q, 8),
        lambda ring, mate: mate * 4 + ring,
        lambda i: (row, div(i, 4) * 8 + rem(i, 4) * 2 + c),
        lambda ref, i: ref.at[i],
        lambda ref, i, h: ref.at[i, pl.ds(4 * h, 4)],
    )
    row_ax = Axis(
        row, div(row, 2), rem(row, 2),
        lambda ring, mate: ring * 2 + mate,
        lambda i: (i, q),
        lambda ref, i: ref.at[:, i],
        lambda ref, i, h: ref.at[pl.ds(4 * h, 4), i],
    )
    sibling = (row, q + 1 - 2 * c)

    barrier = pltpu.get_barrier_semaphore()
    for ax in (col_ax, row_ax):
        for d in range(1, 8):
            pl.semaphore_signal(barrier, inc=1, device_id=ax.device(rem(ax.me + d, 8)), device_id_type=MESH)
    pl.semaphore_signal(barrier, inc=1, device_id=sibling, device_id_type=MESH)

    def energies(start):
        return pair_energy(
            order_ref[:, pl.ds(pl.multiple_of(start, 1024), 1024)], occ_ref[...], vir_ref[...]
        )

    row_energy, col_energy = energies(row * 1024), energies(k * 1024)
    for h in range(2):
        mine = row_energy[:, h * 512 : (h + 1) * 512]
        er_ref[h] = jnp.broadcast_to(mine, (128, 512)).T
        ec_ref[h] = col_energy[:, h * 512 : (h + 1) * 512]
    pl.semaphore_wait(barrier, 15)

    used = [0, 0]
    pending = {}

    def send(src, dst, device):
        i = used[0]
        used[0] += 1
        copy = pltpu.make_async_remote_copy(
            src_ref=src, dst_ref=dst, send_sem=ss.at[i], recv_sem=rs.at[i],
            device_id=device, device_id_type=MESH,
        )
        copy.start()
        pending[id(copy)] = copy
        return copy

    def local(src, dst):
        i = used[1]
        used[1] += 1
        copy = pltpu.make_async_copy(src, dst, ls.at[i])
        copy.start()
        return copy

    def sent(copies):
        for copy in copies:
            if pending.pop(id(copy), None) is not None:
                copy.wait_send()

    def all_to_all(ax, src, dst):
        mine = local(src(ax.me), dst(ax.me))
        copies = []
        for d in (4, 3, 5, 2, 6, 1, 7):
            to = rem(ax.me + d, 8)
            copies.append(send(src(to), dst(ax.me), ax.device(to)))

        def wait():
            for copy in copies:
                copy.wait_recv()
            mine.wait()

        return wait

    class Drip:
        def __init__(self, ax, src, dst):
            self.ax, self.src, self.dst = ax, src, dst
            self.mine = local(src(ax.me), dst(ax.me))
            self.left, self.copies = [4, 3, 5, 2, 6, 1, 7], []

        def __call__(self, n):
            for d in self.left[:n]:
                to = rem(self.ax.me + d, 8)
                self.copies.append(send(self.src(to), self.dst(self.ax.me), self.ax.device(to)))
            self.left = self.left[n:]

        def wait(self):
            for copy in self.copies:
                copy.wait_recv()
            self.mine.wait()

    class Scatter:
        def __init__(self, ax, part, far, near, stage, mate_land):
            self.ax, self.part, self.far, self.near = ax, part, far, near
            self.stage, self.mate_land = stage, mate_land
            self.far_copies, self.near_copies = [None, None], [None, None]

        def at(self, d, m):
            mate = (1 - self.ax.mate) if m == 0 else self.ax.mate
            return self.ax.index(rem(self.ax.ring + d, 4), mate)

        def next(self, d):
            return self.ax.device(self.ax.index(rem(self.ax.ring + d, 4), self.ax.mate))

        def start(self, m):
            self.far_copies[m] = [
                send(self.ax.half(self.part, self.at(2, m), h), self.far.at[m, h], self.next((1, 3)[h]))
                for h in range(2)
            ]

        def step(self, m):
            self.near_copies[m] = []
            for h in range(2):
                d = (1, 3)[h]
                self.far_copies[m][h].wait_recv()
                half = self.ax.half(self.part, self.at(d, m), h)
                half[...] = half[...] + self.far[m, h]
                self.near_copies[m].append(
                    send(self.ax.pick(self.part, self.at(d, m)), self.near.at[m, h], self.next(d))
                )

        def total(self, m):
            for copy in self.near_copies[m]:
                copy.wait_recv()
            return self.ax.pick(self.part, self.at(0, m))[...] + (self.near[m, 0] + self.near[m, 1])

        def to_mate(self):
            self.stage[...] = self.total(0)
            self.mate_copy = send(self.stage, self.mate_land, self.ax.device(self.at(0, 0)))

        def end(self):
            value = self.total(1)
            self.mate_copy.wait_recv()
            return value + self.mate_land[...]

        def copies(self):
            return sum(self.far_copies + self.near_copies, []) + [self.mate_copy]

    class Gather:
        def __init__(self, ax, full, also=None):
            self.ax, self.full = ax, full
            self.also = also if also is not None else (lambda i: None)

        def at(self, d, m):
            mate = (1 - self.ax.mate) if m == 0 else self.ax.mate
            return self.ax.index(rem(self.ax.ring + d, 4), mate)

        def both_ways(self, m):
            piece = self.ax.pick(self.full, self.at(0, m))
            self.also(self.at(0, m))
            return [send(piece, piece, self.ax.device(self.at(d, 1))) for d in (1, 3)]

        def onward(self, m, copies):
            out = []
            for h in range(2):
                copies[h].wait_recv()
                i = self.at((3, 1)[h], m)
                piece = self.ax.half(self.full, i, h)
                out.append(send(piece, piece, self.ax.device(self.at((1, 3)[h], 1))))
                self.also(i)
            return out

        def start(self):
            piece = self.ax.pick(self.full, self.ax.me)
            self.mate_copy = send(piece, piece, self.ax.device(self.at(0, 0)))
            self.own = self.both_ways(1)

        def step1(self):
            self.own_far = self.onward(1, self.own)

        def step2(self):
            self.mate_copy.wait_recv()
            self.other = self.both_ways(0)

        def step3(self):
            self.other_far = self.onward(0, self.other)

        def end(self):
            for m, copies in ((1, self.own_far), (0, self.other_far)):
                for copy in copies:
                    copy.wait_recv()
                self.also(self.at(2, m))

    def lanes(n, size):
        return pl.ds(pl.multiple_of(n * size, size), size)

    a_copy = send(a_ref.at[o], a_in, sibling)
    f_copy = send(f_ref, f_sib, sibling)
    f_mine = local(f_ref.at[row], fg.at[k])
    f_mine.wait()
    f_gather = Gather(col_ax, fg)
    f_gather.start()
    v_hop1 = all_to_all(row_ax, lambda i: v_ref.at[:, i], lambda i: b1.at[i])

    fk_hl[0, c], fk_hl[1, c] = split(f_ref[...].reshape(512, 1024))
    lh[0, :, lanes(c, 512)], lh[1, :, lanes(c, 512)] = split(a_ref[c])
    a_copy.wait_recv()
    lh[0, :, lanes(o, 512)], lh[1, :, lanes(o, 512)] = split(a_in[...])
    f_copy.wait_recv()
    fk_hl[0, o], fk_hl[1, o] = split(f_sib[...].reshape(512, 1024))
    f_gather.step1()
    f_gather.step2()

    def chunk(ref, h):
        return ref.at[(slice(None),) * (len(ref.shape) - 1) + (pl.ds(h * 512, 512),)]

    def product_nn(left, right, out, h):
        @pl.loop(0, 2)
        def _(n):
            cols = pl.ds(pl.multiple_of(h * 512 + n * 256, 256), 256)
            res = triple(
                dot_nn, left[0], left[1],
                right[0, :, :, cols].reshape(1024, 256), right[1, :, :, cols].reshape(1024, 256),
            )
            out[:, :, :, cols] = res.reshape(8, 8, 8, 256)

    def scatters(ax, part, far, near, stage, mate_land):
        return [
            Scatter(ax, chunk(part, h), far.at[h], near.at[h], stage.at[h], mate_land.at[h]) for h in range(2)
        ]

    rs0 = scatters(col_ax, pa, far_c, near_c, sum_c, mate_c)
    i_gather = [Gather(col_ax, chunk(inter, h)) for h in range(2)]
    for h in range(2):
        product_nn(lh, fk_hl, pa, h)
        rs0[h].start(0)
        rs0[h].start(1)
    f_gather.step3()
    v_copy = send(v_ref.at[o], v_in, sibling)
    rs0[0].step(0)
    rs0[0].step(1)
    rs0[0].to_mate()
    rs0[1].step(0)
    f_gather.end()

    def start_inter(h):
        chunk(inter, h)[k] = rs0[h].end()
        i_gather[h].start()

    start_inter(0)
    rs0[1].step(1)
    rs0[1].to_mate()
    i_gather[0].step1()
    i_gather[0].step2()
    start_inter(1)
    i_gather[0].step3()
    i_gather[1].step1()
    i_gather[1].step2()
    f_hop = all_to_all(row_ax, lambda i: fg.at[i], lambda i: fr.at[c, i])
    i_gather[0].end()
    lf[0, :, :512], lf[1, :, :512] = split(inter[:, :, :, :512].reshape(512, 512))
    i_gather[1].step3()
    i_gather[1].end()
    lf[0, :, 512:], lf[1, :, 512:] = split(inter[:, :, :, 512:].reshape(512, 512))
    v_hop1()
    v_hop2 = all_to_all(col_ax, lambda i: b1.at[i], lambda i: b2.at[i])

    v_copy.wait_recv()

    @pl.loop(0, 2)
    def _(n):
        rows = lanes(n, 256)
        res = triple(dot_nt, lf[0], lf[1], fk_hl[0, o, rows], fk_hl[1, o, rows])
        drive = v_in[:, :, rows].reshape(512, 256)
        y = (drive + res) / (er_ref[c, :, :1] + ec_ref[o, :, rows])
        y_out[:, rows] = y
        at = pl.ds(pl.multiple_of(o * 512 + n * 256, 256), 256)
        lh[0, :, at], lh[1, :, at] = split(y)

    y_copy = send(y_out, y_in, sibling)

    @pl.loop(0, 2)
    def _(n):
        rows = lanes(n, 256)
        res = triple(dot_nt, lf[0], lf[1], fk_hl[0, c, rows], fk_hl[1, c, rows])
        drive = v_ref[c, :, :, rows].reshape(512, 256)
        y = (drive + res) / (er_ref[c, :, :1] + ec_ref[c, :, rows])
        at = pl.ds(pl.multiple_of(c * 512 + n * 256, 256), 256)
        lh[0, :, at], lh[1, :, at] = split(y)
        lt[0, rows, lanes(c, 512)], lt[1, rows, lanes(c, 512)] = split(y.T)

    f_hop()
    f_copy2 = send(fr.at[c], fr.at[c], sibling)
    sent(rs0[0].copies() + rs0[1].copies())
    rs1_c = scatters(col_ax, pa, far_c, near_c, sum_c, mate_c)
    rs1_r = scatters(row_ax, pb, far_r, near_r, sum_r, mate_r)
    for h in range(2):
        product_nn(lh, fk_hl, pa, h)
        rs1_c[h].start(0)
        rs1_c[h].start(1)
    y_copy.wait_recv()

    @pl.loop(0, 2)
    def _(n):
        rows = lanes(n, 256)
        lt[0, rows, lanes(o, 512)], lt[1, rows, lanes(o, 512)] = split(y_in[:, rows].T)

    fr_hl[0, c], fr_hl[1, c] = split(fr[c].reshape(512, 1024))
    f_copy2.wait_recv()
    fr_hl[0, o], fr_hl[1, o] = split(fr[o].reshape(512, 1024))
    for h in range(2):
        product_nn(lt, fr_hl, pb, h)
        rs1_r[h].start(0)
        rs1_r[h].start(1)
        if h == 0:
            rs1_c[0].step(0)
            rs1_c[0].step(1)

    c_hop1, r_hop1, c_hop2, r_hop2 = [None] * 2, [None] * 2, [None] * 2, [None] * 2
    k_gather = [Gather(row_ax, chunk(wk, h)) for h in range(2)]
    r_gather = [Gather(col_ax, chunk(wr.at[c], h)) for h in range(2)]

    def end_c(h):
        own_c[h] = (2.0 * KEEP * OMEGA) * chunk(inter, h)[k] - (OMEGA * OMEGA) * rs1_c[h].end()
        c_hop1[h] = all_to_all(row_ax, lambda i: own_c.at[h, i], lambda i: t1.at[h, i])

    def end_r(h):
        own_r[h] = -(OMEGA * OMEGA) * rs1_r[h].end()
        r_hop1[h] = all_to_all(col_ax, lambda i: own_r.at[h, i], lambda i: u1.at[h, i])

    def second_hops(h):
        c_hop1[h]()
        c_hop2[h] = all_to_all(col_ax, lambda i: t1.at[h, i], lambda i: t2.at[h, i])
        r_hop1[h]()
        r_hop2[h] = all_to_all(row_ax, lambda i: u1.at[h, i], lambda i: u2.at[h, i])

    def start_gathers(h):
        c_hop2[h]()
        row_ax.pick(chunk(wk, h), row)[...] = own_r[h] + t2[h]
        k_gather[h].start()
        r_hop2[h]()
        col_ax.pick(chunk(wr.at[c], h), k)[...] = own_c[h] + u2[h]
        r_gather[h].start()

    rs1_c[0].to_mate()
    rs1_c[1].step(0)
    rs1_r[0].step(0)
    rs1_r[0].step(1)
    end_c(0)
    rs1_c[1].step(1)
    rs1_r[0].to_mate()
    rs1_r[1].step(0)
    rs1_c[1].to_mate()
    end_r(0)
    rs1_r[1].step(1)
    end_c(1)
    rs1_r[1].to_mate()
    second_hops(0)
    end_r(1)
    start_gathers(0)
    v_hop2()
    v_hop3 = Drip(row_ax, lambda i: b2.at[i], lambda i: b3.at[i])
    v_hop3(2)
    second_hops(1)
    for gather in (k_gather[0], r_gather[0]):
        gather.step1()
        gather.step2()
    start_gathers(1)
    v_hop3(1)
    v_hop3(2)
    k_gather[0].step3()
    r_gather[0].step3()
    v_hop3(2)
    for gather in (k_gather[1], r_gather[1]):
        gather.step1()
        gather.step2()

    def take(h):
        cols = pl.ds(h * 512, 512)
        copy = send(chunk(wr.at[c], h), chunk(wr.at[c], h), sibling)
        lf[0, :, cols], lf[1, :, cols] = split(wr[c, :, :, :, cols].reshape(512, 512))
        lt[0, :, cols], lt[1, :, cols] = split(wk[:, :, :, cols].reshape(512, 512))
        return copy

    def take_sibling(h, copy):
        cols = pl.ds(h * 512, 512)
        copy.wait_recv()
        lh[0, :, cols], lh[1, :, cols] = split(wr[o, :, :, :, cols].reshape(512, 512))

    def terms(half, left, n, h):
        rows, cols = lanes(n, 256), pl.ds(h * 512, 512)
        return triple(
            dot_nt, left[0, :, cols], left[1, :, cols], fk_hl[0, c, rows, cols], fk_hl[1, c, rows, cols]
        ) + triple(
            dot_nt, fr_hl[0, half, :, cols], fr_hl[1, half, :, cols], lt[0, rows, cols], lt[1, rows, cols]
        )

    def first(half, left):
        @pl.loop(0, 2)
        def _(n):
            o_ref[half, :, lanes(n, 256)] = terms(half, left, n, 0)

    k_gather[0].end()
    r_gather[0].end()
    w_copy = take(0)
    k_gather[1].step3()
    r_gather[1].step3()
    first(c, lf)
    take_sibling(0, w_copy)
    first(o, lh)
    v_hop3.wait()
    vt_copy = send(b3.at[:, o], vt_sib, sibling)
    k_gather[1].end()
    r_gather[1].end()
    w_copy = take(1)

    def finish(half, left, mirrored):
        @pl.loop(0, 2)
        def _(n):
            rows = lanes(n, 256)
            res = o_ref[half, :, rows] + terms(half, left, n, 1)
            drive = v_ref[half, :, :, rows].reshape(512, 256) + mirrored(n).reshape(256, 512).T
            sym = (1.0 + KEEP) * OMEGA * drive + res
            o_ref[half, :, rows] = (KEEP * KEEP) * a_ref[half, :, rows] - sym / (
                er_ref[half, :, :1] + ec_ref[c, :, rows]
            )

    finish(c, lf, lambda n: b3[pl.ds(n * 4, 4), c])
    take_sibling(1, w_copy)
    vt_copy.wait_recv()
    finish(o, lh, lambda n: vt_sib[pl.ds(n * 4, 4)])
    sent(list(pending.values()))


def on_device(amplitudes, integrals, factors, pair_order, occ_energy, vir_energy):
    big = lambda *shape: pltpu.VMEM(shape, F32)
    half = lambda *shape: pltpu.VMEM(shape, BF16)
    out = pl.pallas_call(
        kernel,
        out_shape=jax.ShapeDtypeStruct((2, 512, 512), F32),
        in_specs=[pl.BlockSpec(memory_space=pltpu.VMEM)] * 6,
        out_specs=pl.BlockSpec(memory_space=pltpu.VMEM),
        scratch_shapes=[
            big(512, 512),
            big(8, 64, 512),
            big(8, 8, 8, 1024),
            half(2, 2, 512, 1024),
            big(2, 8, 8, 8, 1024),
            half(2, 2, 512, 1024),
            big(8, 8, 8, 1024),
            big(2, 2, 2, 4, 8, 512),
            big(2, 2, 2, 8, 8, 512),
            big(2, 2, 2, 4, 8, 512),
            big(2, 2, 2, 8, 8, 512),
            big(2, 8, 8, 512),
            big(2, 8, 8, 512),
            big(2, 8, 8, 512),
            big(2, 8, 8, 512),
            big(2, 8, 8, 512),
            big(2, 8, 8, 512),
            big(8, 8, 8, 1024),
            big(512, 512),
            half(2, 512, 1024),
            half(2, 512, 1024),
            half(2, 512, 1024),
            big(2, 8, 8, 8, 1024),
            big(8, 8, 8, 1024),
            big(8, 2, 64, 512),
            big(8, 2, 64, 512),
            big(8, 2, 64, 512),
            big(8, 64, 512),
            big(2, 8, 8, 512),
            big(2, 8, 8, 512),
            big(2, 8, 8, 512),
            big(2, 8, 8, 512),
            big(8, 8, 8, 1024),
            big(2, 512, 128),
            big(2, 1, 512),
            pltpu.SemaphoreType.DMA((N_SEM,)),
            pltpu.SemaphoreType.DMA((N_SEM,)),
            pltpu.SemaphoreType.DMA((16,)),
        ],
        compiler_params=pltpu.CompilerParams(
            collective_id=0, has_side_effects=True, vmem_limit_bytes=63 * 2**20
        ),
        name="lambda_steps",
    )(
        amplitudes.reshape(2, 512, 512),
        integrals.reshape(2, 8, 64, 512),
        factors.reshape(8, 8, 8, 1024),
        pair_order.reshape(1, NO * NV),
        occ_energy.reshape(NO, 1),
        vir_energy.reshape(NV, 1),
    )
    return out.reshape(1024, 512)


def solution(mesh):
    return jax.shard_map(
        on_device,
        mesh=mesh,
        in_specs=(P("row", "col"), P("row", "col"), P("col", None), P(), P(), P()),
        out_specs=P("row", "col"),
        check_vma=False,
    )
```

```python
import jax
import jax.numpy as jnp
from jax import lax
from jax.experimental import pallas as pl
from jax.experimental.pallas import tpu as pltpu
from jax.sharding import PartitionSpec as P

NO = 64
NV = 128
OMEGA = 0.6
KEEP = 1.0 - OMEGA

MESH = pl.DeviceIdType.MESH
F32 = jnp.float32
BF16 = jnp.bfloat16
N_SEM = 232


def upright(line):
    n = line.shape[1]
    here = lax.broadcasted_iota(jnp.int32, (n, n), 0) == lax.broadcasted_iota(jnp.int32, (n, n), 1)
    return jnp.sum(jnp.where(here, line, 0.0), axis=1, keepdims=True)


def pair_energy(codes, occ, vir):
    n = codes.shape[1]
    occ, vir = upright(occ), upright(vir)
    at_occ = lax.broadcasted_iota(jnp.int32, (NO, n), 0)
    at_vir = lax.broadcasted_iota(jnp.int32, (NV, n), 0)
    occ_hit = at_occ == lax.shift_right_logical(codes, jnp.int32(7))
    vir_hit = at_vir == (codes & (NV - 1))
    return jnp.sum(jnp.where(vir_hit, vir, 0.0), axis=0, keepdims=True) - jnp.sum(
        jnp.where(occ_hit, occ, 0.0), axis=0, keepdims=True
    )


def rem(a, b):
    return lax.rem(a, jnp.int32(b))


def div(a, b):
    return lax.div(a, jnp.int32(b))


def split(value):
    high = value.astype(BF16)
    return high, (value - high.astype(F32)).astype(BF16)


def dot_nn(a, b):
    return lax.dot_general(a, b, (((1,), (0,)), ((), ())), preferred_element_type=F32)


def dot_nt(a, b):
    return lax.dot_general(a, b, (((1,), (1,)), ((), ())), preferred_element_type=F32)


def triple(dot, ah, al, bh, bl):
    return dot(ah, bh) + (dot(ah, bl) + dot(al, bh))


class Axis:
    def __init__(self, me, ring, mate, index, device, pick, half):
        self.me, self.ring, self.mate = me, ring, mate
        self.index, self.device, self.pick, self.half = index, device, pick, half


def kernel(
    a_ref, v_ref, f_ref, order_ref, occ_ref, vir_ref, o_ref,
    a_in, v_in, f_sib, fk_hl, fr, fr_hl, pa, far_c, near_c, far_r, near_r, mate_c, mate_r,
    sum_c, sum_r, own_c, own_r, inter, y_in, lh, lf, lt, wr, wk,
    b1, b2, b3, vt_sib, t1, t2, u1, u2, fg, er_ref, ec_ref, ss, rs, ls,
):
    pb, y_out = f_sib, a_in
    row = lax.axis_index("row")
    q = lax.axis_index("col")
    c = rem(q, 2)
    o = 1 - c
    k = div(q, 8) * 4 + rem(div(q, 2), 4)
    col_ax = Axis(
        k, rem(div(q, 2), 4), div(q, 8),
        lambda ring, mate: mate * 4 + ring,
        lambda i: (row, div(i, 4) * 8 + rem(i, 4) * 2 + c),
        lambda ref, i: ref.at[i],
        lambda ref, i, h: ref.at[i, pl.ds(4 * h, 4)],
    )
    row_ax = Axis(
        row, div(row, 2), rem(row, 2),
        lambda ring, mate: ring * 2 + mate,
        lambda i: (i, q),
        lambda ref, i: ref.at[:, i],
        lambda ref, i, h: ref.at[pl.ds(4 * h, 4), i],
    )
    sibling = (row, q + 1 - 2 * c)

    barrier = pltpu.get_barrier_semaphore()
    for ax in (col_ax, row_ax):
        for d in range(1, 8):
            pl.semaphore_signal(barrier, inc=1, device_id=ax.device(rem(ax.me + d, 8)), device_id_type=MESH)
    pl.semaphore_signal(barrier, inc=1, device_id=sibling, device_id_type=MESH)

    def energies(start):
        return pair_energy(
            order_ref[:, pl.ds(pl.multiple_of(start, 1024), 1024)], occ_ref[...], vir_ref[...]
        )

    row_energy, col_energy = energies(row * 1024), energies(k * 1024)
    for h in range(2):
        mine = row_energy[:, h * 512 : (h + 1) * 512]
        er_ref[h] = jnp.broadcast_to(mine, (128, 512)).T
        ec_ref[h] = col_energy[:, h * 512 : (h + 1) * 512]
    pl.semaphore_wait(barrier, 15)

    used = [0, 0]
    pending = {}

    def send(src, dst, device):
        i = used[0]
        used[0] += 1
        copy = pltpu.make_async_remote_copy(
            src_ref=src, dst_ref=dst, send_sem=ss.at[i], recv_sem=rs.at[i],
            device_id=device, device_id_type=MESH,
        )
        copy.start()
        pending[id(copy)] = copy
        return copy

    def local(src, dst):
        i = used[1]
        used[1] += 1
        copy = pltpu.make_async_copy(src, dst, ls.at[i])
        copy.start()
        return copy

    def sent(copies):
        for copy in copies:
            if pending.pop(id(copy), None) is not None:
                copy.wait_send()

    def all_to_all(ax, src, dst):
        mine = local(src(ax.me), dst(ax.me))
        copies = []
        for d in (4, 3, 5, 2, 6, 1, 7):
            to = rem(ax.me + d, 8)
            copies.append(send(src(to), dst(ax.me), ax.device(to)))

        def wait():
            for copy in copies:
                copy.wait_recv()
            mine.wait()

        return wait

    class Drip:
        def __init__(self, ax, src, dst):
            self.ax, self.src, self.dst = ax, src, dst
            self.mine = local(src(ax.me), dst(ax.me))
            self.left, self.copies = [4, 3, 5, 2, 6, 1, 7], []

        def __call__(self, n):
            for d in self.left[:n]:
                to = rem(self.ax.me + d, 8)
                self.copies.append(send(self.src(to), self.dst(self.ax.me), self.ax.device(to)))
            self.left = self.left[n:]

        def wait(self):
            for copy in self.copies:
                copy.wait_recv()
            self.mine.wait()

    class Scatter:
        def __init__(self, ax, part, far, near, stage, mate_land):
            self.ax, self.part, self.far, self.near = ax, part, far, near
            self.stage, self.mate_land = stage, mate_land
            self.far_copies, self.near_copies = [None, None], [None, None]

        def at(self, d, m):
            mate = (1 - self.ax.mate) if m == 0 else self.ax.mate
            return self.ax.index(rem(self.ax.ring + d, 4), mate)

        def next(self, d):
            return self.ax.device(self.ax.index(rem(self.ax.ring + d, 4), self.ax.mate))

        def start(self, m):
            self.far_copies[m] = [
                send(self.ax.half(self.part, self.at(2, m), h), self.far.at[m, h], self.next((1, 3)[h]))
                for h in range(2)
            ]

        def step(self, m):
            self.near_copies[m] = []
            for h in range(2):
                d = (1, 3)[h]
                self.far_copies[m][h].wait_recv()
                half = self.ax.half(self.part, self.at(d, m), h)
                half[...] = half[...] + self.far[m, h]
                self.near_copies[m].append(
                    send(self.ax.pick(self.part, self.at(d, m)), self.near.at[m, h], self.next(d))
                )

        def total(self, m):
            for copy in self.near_copies[m]:
                copy.wait_recv()
            return self.ax.pick(self.part, self.at(0, m))[...] + (self.near[m, 0] + self.near[m, 1])

        def to_mate(self):
            self.stage[...] = self.total(0)
            self.mate_copy = send(self.stage, self.mate_land, self.ax.device(self.at(0, 0)))

        def end(self):
            value = self.total(1)
            self.mate_copy.wait_recv()
            return value + self.mate_land[...]

        def copies(self):
            return sum(self.far_copies + self.near_copies, []) + [self.mate_copy]

    class Gather:
        def __init__(self, ax, full, also=None):
            self.ax, self.full = ax, full
            self.also = also if also is not None else (lambda i: None)

        def at(self, d, m):
            mate = (1 - self.ax.mate) if m == 0 else self.ax.mate
            return self.ax.index(rem(self.ax.ring + d, 4), mate)

        def both_ways(self, m):
            piece = self.ax.pick(self.full, self.at(0, m))
            self.also(self.at(0, m))
            return [send(piece, piece, self.ax.device(self.at(d, 1))) for d in (1, 3)]

        def onward(self, m, copies):
            out = []
            for h in range(2):
                copies[h].wait_recv()
                i = self.at((3, 1)[h], m)
                piece = self.ax.half(self.full, i, h)
                out.append(send(piece, piece, self.ax.device(self.at((1, 3)[h], 1))))
                self.also(i)
            return out

        def start(self):
            piece = self.ax.pick(self.full, self.ax.me)
            self.mate_copy = send(piece, piece, self.ax.device(self.at(0, 0)))
            self.own = self.both_ways(1)

        def step1(self):
            self.own_far = self.onward(1, self.own)

        def step2(self):
            self.mate_copy.wait_recv()
            self.other = self.both_ways(0)

        def step3(self):
            self.other_far = self.onward(0, self.other)

        def end(self):
            for m, copies in ((1, self.own_far), (0, self.other_far)):
                for copy in copies:
                    copy.wait_recv()
                self.also(self.at(2, m))

    def lanes(n, size):
        return pl.ds(pl.multiple_of(n * size, size), size)

    a_copy = send(a_ref.at[o], a_in, sibling)
    f_copy = send(f_ref, f_sib, sibling)
    f_mine = local(f_ref.at[row], fg.at[k])
    f_mine.wait()
    f_gather = Gather(col_ax, fg)
    f_gather.start()
    v_hop1 = all_to_all(row_ax, lambda i: v_ref.at[:, i], lambda i: b1.at[i])

    fk_hl[0, c], fk_hl[1, c] = split(f_ref[...].reshape(512, 1024))
    lh[0, :, lanes(c, 512)], lh[1, :, lanes(c, 512)] = split(a_ref[c])
    a_copy.wait_recv()
    lh[0, :, lanes(o, 512)], lh[1, :, lanes(o, 512)] = split(a_in[...])
    f_copy.wait_recv()
    fk_hl[0, o], fk_hl[1, o] = split(f_sib[...].reshape(512, 1024))
    f_gather.step1()
    f_gather.step2()

    def chunk(ref, h):
        return ref.at[(slice(None),) * (len(ref.shape) - 1) + (pl.ds(h * 512, 512),)]

    def product_nn(left, right, out, h):
        @pl.loop(0, 2)
        def _(n):
            cols = pl.ds(pl.multiple_of(h * 512 + n * 256, 256), 256)
            res = triple(
                dot_nn, left[0], left[1],
                right[0, :, :, cols].reshape(1024, 256), right[1, :, :, cols].reshape(1024, 256),
            )
            out[:, :, :, cols] = res.reshape(8, 8, 8, 256)

    def scatters(ax, part, far, near, stage, mate_land):
        return [
            Scatter(ax, chunk(part, h), far.at[h], near.at[h], stage.at[h], mate_land.at[h]) for h in range(2)
        ]

    rs0 = scatters(col_ax, pa, far_c, near_c, sum_c, mate_c)
    i_gather = [Gather(col_ax, chunk(inter, h)) for h in range(2)]
    for h in range(2):
        product_nn(lh, fk_hl, pa, h)
        rs0[h].start(0)
        rs0[h].start(1)
    f_gather.step3()
    v_copy = send(v_ref.at[o], v_in, sibling)
    rs0[0].step(0)
    rs0[0].step(1)
    rs0[0].to_mate()
    rs0[1].step(0)
    f_gather.end()

    def start_inter(h):
        chunk(inter, h)[k] = rs0[h].end()
        i_gather[h].start()

    start_inter(0)
    rs0[1].step(1)
    rs0[1].to_mate()
    i_gather[0].step1()
    i_gather[0].step2()
    start_inter(1)
    i_gather[0].step3()
    i_gather[1].step1()
    i_gather[1].step2()
    f_hop = all_to_all(row_ax, lambda i: fg.at[i], lambda i: fr.at[c, i])
    i_gather[0].end()
    lf[0, :, :512], lf[1, :, :512] = split(inter[:, :, :, :512].reshape(512, 512))
    i_gather[1].step3()
    i_gather[1].end()
    lf[0, :, 512:], lf[1, :, 512:] = split(inter[:, :, :, 512:].reshape(512, 512))
    v_hop1()
    v_hop2 = all_to_all(col_ax, lambda i: b1.at[i], lambda i: b2.at[i])

    v_copy.wait_recv()

    @pl.loop(0, 2)
    def _(n):
        rows = lanes(n, 256)
        res = triple(dot_nt, lf[0], lf[1], fk_hl[0, o, rows], fk_hl[1, o, rows])
        drive = v_in[:, :, rows].reshape(512, 256)
        y = (drive + res) / (er_ref[c, :, :1] + ec_ref[o, :, rows])
        y_out[:, rows] = y
        at = pl.ds(pl.multiple_of(o * 512 + n * 256, 256), 256)
        lh[0, :, at], lh[1, :, at] = split(y)

    y_copy = send(y_out, y_in, sibling)

    @pl.loop(0, 2)
    def _(n):
        rows = lanes(n, 256)
        res = triple(dot_nt, lf[0], lf[1], fk_hl[0, c, rows], fk_hl[1, c, rows])
        drive = v_ref[c, :, :, rows].reshape(512, 256)
        y = (drive + res) / (er_ref[c, :, :1] + ec_ref[c, :, rows])
        at = pl.ds(pl.multiple_of(c * 512 + n * 256, 256), 256)
        lh[0, :, at], lh[1, :, at] = split(y)
        lt[0, rows, lanes(c, 512)], lt[1, rows, lanes(c, 512)] = split(y.T)

    f_hop()
    f_copy2 = send(fr.at[c], fr.at[c], sibling)
    sent(rs0[0].copies() + rs0[1].copies())
    rs1_c = scatters(col_ax, pa, far_c, near_c, sum_c, mate_c)
    rs1_r = scatters(row_ax, pb, far_r, near_r, sum_r, mate_r)
    for h in range(2):
        product_nn(lh, fk_hl, pa, h)
        rs1_c[h].start(0)
        rs1_c[h].start(1)
    y_copy.wait_recv()

    @pl.loop(0, 2)
    def _(n):
        rows = lanes(n, 256)
        lt[0, rows, lanes(o, 512)], lt[1, rows, lanes(o, 512)] = split(y_in[:, rows].T)

    fr_hl[0, c], fr_hl[1, c] = split(fr[c].reshape(512, 1024))
    f_copy2.wait_recv()
    fr_hl[0, o], fr_hl[1, o] = split(fr[o].reshape(512, 1024))
    for h in range(2):
        product_nn(lt, fr_hl, pb, h)
        rs1_r[h].start(0)
        rs1_r[h].start(1)
        if h == 0:
            rs1_c[0].step(0)
            rs1_c[0].step(1)

    c_hop1, r_hop1, c_hop2, r_hop2 = [None] * 2, [None] * 2, [None] * 2, [None] * 2
    k_gather = [Gather(row_ax, chunk(wk, h)) for h in range(2)]
    r_gather = [Gather(col_ax, chunk(wr.at[c], h)) for h in range(2)]

    def end_c(h):
        own_c[h] = (2.0 * KEEP * OMEGA) * chunk(inter, h)[k] - (OMEGA * OMEGA) * rs1_c[h].end()
        c_hop1[h] = all_to_all(row_ax, lambda i: own_c.at[h, i], lambda i: t1.at[h, i])

    def end_r(h):
        own_r[h] = -(OMEGA * OMEGA) * rs1_r[h].end()
        r_hop1[h] = all_to_all(col_ax, lambda i: own_r.at[h, i], lambda i: u1.at[h, i])

    def second_hops(h):
        c_hop1[h]()
        c_hop2[h] = all_to_all(col_ax, lambda i: t1.at[h, i], lambda i: t2.at[h, i])
        r_hop1[h]()
        r_hop2[h] = all_to_all(row_ax, lambda i: u1.at[h, i], lambda i: u2.at[h, i])

    def start_gathers(h):
        c_hop2[h]()
        row_ax.pick(chunk(wk, h), row)[...] = own_r[h] + t2[h]
        k_gather[h].start()
        r_hop2[h]()
        col_ax.pick(chunk(wr.at[c], h), k)[...] = own_c[h] + u2[h]
        r_gather[h].start()

    rs1_c[0].to_mate()
    rs1_c[1].step(0)
    rs1_r[0].step(0)
    rs1_r[0].step(1)
    end_c(0)
    rs1_c[1].step(1)
    rs1_r[0].to_mate()
    rs1_r[1].step(0)
    rs1_c[1].to_mate()
    end_r(0)
    rs1_r[1].step(1)
    end_c(1)
    rs1_r[1].to_mate()
    second_hops(0)
    end_r(1)
    start_gathers(0)
    v_hop2()
    v_hop3 = Drip(row_ax, lambda i: b2.at[i], lambda i: b3.at[i])
    v_hop3(2)
    second_hops(1)
    for gather in (k_gather[0], r_gather[0]):
        gather.step1()
        gather.step2()
    start_gathers(1)
    v_hop3(1)
    v_hop3(2)
    k_gather[0].step3()
    r_gather[0].step3()
    v_hop3(2)
    for gather in (k_gather[1], r_gather[1]):
        gather.step1()
        gather.step2()

    def take(h):
        cols = pl.ds(h * 512, 512)
        copy = send(chunk(wr.at[c], h), chunk(wr.at[c], h), sibling)
        lf[0, :, cols], lf[1, :, cols] = split(wr[c, :, :, :, cols].reshape(512, 512))
        lt[0, :, cols], lt[1, :, cols] = split(wk[:, :, :, cols].reshape(512, 512))
        return copy

    def take_sibling(h, copy):
        cols = pl.ds(h * 512, 512)
        copy.wait_recv()
        lh[0, :, cols], lh[1, :, cols] = split(wr[o, :, :, :, cols].reshape(512, 512))

    def terms(half, left, n, h):
        rows, cols = lanes(n, 256), pl.ds(h * 512, 512)
        return triple(
            dot_nt, left[0, :, cols], left[1, :, cols], fk_hl[0, c, rows, cols], fk_hl[1, c, rows, cols]
        ) + triple(
            dot_nt, fr_hl[0, half, :, cols], fr_hl[1, half, :, cols], lt[0, rows, cols], lt[1, rows, cols]
        )

    def first(half, left):
        @pl.loop(0, 2)
        def _(n):
            o_ref[half, :, lanes(n, 256)] = terms(half, left, n, 0)

    k_gather[0].end()
    r_gather[0].end()
    w_copy = take(0)
    k_gather[1].step3()
    r_gather[1].step3()
    first(c, lf)
    take_sibling(0, w_copy)
    first(o, lh)
    v_hop3.wait()
    vt_copy = send(b3.at[:, o], vt_sib, sibling)
    k_gather[1].end()
    r_gather[1].end()
    w_copy = take(1)

    def finish(half, left, mirrored):
        @pl.loop(0, 2)
        def _(n):
            rows = lanes(n, 256)
            res = o_ref[half, :, rows] + terms(half, left, n, 1)
            drive = v_ref[half, :, :, rows].reshape(512, 256) + mirrored(n).reshape(256, 512).T
            sym = (1.0 + KEEP) * OMEGA * drive + res
            o_ref[half, :, rows] = (KEEP * KEEP) * a_ref[half, :, rows] - sym / (
                er_ref[half, :, :1] + ec_ref[c, :, rows]
            )

    finish(c, lf, lambda n: b3[pl.ds(n * 4, 4), c])
    take_sibling(1, w_copy)
    vt_copy.wait_recv()
    finish(o, lh, lambda n: vt_sib[pl.ds(n * 4, 4)])
    sent(list(pending.values()))


def on_device(amplitudes, integrals, factors, pair_order, occ_energy, vir_energy):
    big = lambda *shape: pltpu.VMEM(shape, F32)
    half = lambda *shape: pltpu.VMEM(shape, BF16)
    out = pl.pallas_call(
        kernel,
        out_shape=jax.ShapeDtypeStruct((2, 512, 512), F32),
        in_specs=[pl.BlockSpec(memory_space=pltpu.VMEM)] * 6,
        out_specs=pl.BlockSpec(memory_space=pltpu.VMEM),
        scratch_shapes=[
            big(512, 512),
            big(8, 64, 512),
            big(8, 8, 8, 1024),
            half(2, 2, 512, 1024),
            big(2, 8, 8, 8, 1024),
            half(2, 2, 512, 1024),
            big(8, 8, 8, 1024),
            big(2, 2, 2, 4, 8, 512),
            big(2, 2, 2, 8, 8, 512),
            big(2, 2, 2, 4, 8, 512),
            big(2, 2, 2, 8, 8, 512),
            big(2, 8, 8, 512),
            big(2, 8, 8, 512),
            big(2, 8, 8, 512),
            big(2, 8, 8, 512),
            big(2, 8, 8, 512),
            big(2, 8, 8, 512),
            big(8, 8, 8, 1024),
            big(512, 512),
            half(2, 512, 1024),
            half(2, 512, 1024),
            half(2, 512, 1024),
            big(2, 8, 8, 8, 1024),
            big(8, 8, 8, 1024),
            big(8, 2, 64, 512),
            big(8, 2, 64, 512),
            big(8, 2, 64, 512),
            big(8, 64, 512),
            big(2, 8, 8, 512),
            big(2, 8, 8, 512),
            big(2, 8, 8, 512),
            big(2, 8, 8, 512),
            big(8, 8, 8, 1024),
            big(2, 512, 128),
            big(2, 1, 512),
            pltpu.SemaphoreType.DMA((N_SEM,)),
            pltpu.SemaphoreType.DMA((N_SEM,)),
            pltpu.SemaphoreType.DMA((16,)),
        ],
        compiler_params=pltpu.CompilerParams(
            collective_id=0, has_side_effects=True, vmem_limit_bytes=63 * 2**20
        ),
        name="lambda_steps",
    )(
        amplitudes.reshape(2, 512, 512),
        integrals.reshape(2, 8, 64, 512),
        factors.reshape(8, 8, 8, 1024),
        pair_order.reshape(1, NO * NV),
        occ_energy.reshape(1, NO),
        vir_energy.reshape(1, NV),
    )
    return out.reshape(1024, 512)


def solution(mesh):
    return jax.shard_map(
        on_device,
        mesh=mesh,
        in_specs=(P("row", "col"), P("row", "col"), P("col", None), P(), P(), P()),
        out_specs=P("row", "col"),
        check_vma=False,
    )
```

```python
import jax
import jax.numpy as jnp
from jax import lax
from jax.experimental import pallas as pl
from jax.experimental.pallas import tpu as pltpu
from jax.sharding import PartitionSpec as P

NO = 64
NV = 128
OMEGA = 0.6
KEEP = 1.0 - OMEGA

MESH = pl.DeviceIdType.MESH
F32 = jnp.float32
BF16 = jnp.bfloat16
N_SEM = 232


def upright(line):
    n = line.shape[1]
    here = lax.broadcasted_iota(jnp.int32, (n, n), 0) == lax.broadcasted_iota(jnp.int32, (n, n), 1)
    return jnp.sum(jnp.where(here, line, 0.0), axis=1, keepdims=True)


def pair_energy(codes, occ, vir):
    n = codes.shape[1]
    occ, vir = upright(occ), upright(vir)
    at_occ = lax.broadcasted_iota(jnp.int32, (NO, n), 0)
    at_vir = lax.broadcasted_iota(jnp.int32, (NV, n), 0)
    occ_hit = at_occ == lax.shift_right_logical(codes, jnp.int32(7))
    vir_hit = at_vir == (codes & (NV - 1))
    return jnp.sum(jnp.where(vir_hit, vir, 0.0), axis=0, keepdims=True) - jnp.sum(
        jnp.where(occ_hit, occ, 0.0), axis=0, keepdims=True
    )


def rem(a, b):
    return lax.rem(a, jnp.int32(b))


def div(a, b):
    return lax.div(a, jnp.int32(b))


def split(value):
    high = value.astype(BF16)
    return high, (value - high.astype(F32)).astype(BF16)


def dot_nn(a, b):
    return lax.dot_general(a, b, (((1,), (0,)), ((), ())), preferred_element_type=F32)


def dot_nt(a, b):
    return lax.dot_general(a, b, (((1,), (1,)), ((), ())), preferred_element_type=F32)


def triple(dot, ah, al, bh, bl):
    return dot(ah, bh) + (dot(ah, bl) + dot(al, bh))


class Axis:
    def __init__(self, me, ring, mate, index, device, pick, half):
        self.me, self.ring, self.mate = me, ring, mate
        self.index, self.device, self.pick, self.half = index, device, pick, half


def kernel(
    a_ref, v_ref, f_ref, order_ref, occ_ref, vir_ref, o_ref,
    a_in, v_in, f_sib, fk_hl, fr, fr_hl, pa, far_c, near_c, far_r, near_r, mate_c, mate_r,
    sum_c, sum_r, own_c, own_r, inter, y_in, lh, lf, lt, wr, wk,
    b1, b2, b3, vt_sib, t1, t2, u1, u2, fg, er_ref, ec_ref, ss, rs, ls,
):
    pb, y_out = f_sib, a_in
    row = lax.axis_index("row")
    q = lax.axis_index("col")
    c = rem(q, 2)
    o = 1 - c
    k = div(q, 8) * 4 + rem(div(q, 2), 4)
    col_ax = Axis(
        k, rem(div(q, 2), 4), div(q, 8),
        lambda ring, mate: mate * 4 + ring,
        lambda i: (row, div(i, 4) * 8 + rem(i, 4) * 2 + c),
        lambda ref, i: ref.at[i],
        lambda ref, i, h: ref.at[i, pl.ds(4 * h, 4)],
    )
    row_ax = Axis(
        row, div(row, 2), rem(row, 2),
        lambda ring, mate: ring * 2 + mate,
        lambda i: (i, q),
        lambda ref, i: ref.at[:, i],
        lambda ref, i, h: ref.at[pl.ds(4 * h, 4), i],
    )
    sibling = (row, q + 1 - 2 * c)

    barrier = pltpu.get_barrier_semaphore()
    for ax in (col_ax, row_ax):
        for d in range(1, 8):
            pl.semaphore_signal(barrier, inc=1, device_id=ax.device(rem(ax.me + d, 8)), device_id_type=MESH)
    pl.semaphore_signal(barrier, inc=1, device_id=sibling, device_id_type=MESH)

    def energies(start):
        return pair_energy(
            order_ref[:, pl.ds(pl.multiple_of(start, 1024), 1024)], occ_ref[...], vir_ref[...]
        )

    row_energy, col_energy = energies(row * 1024), energies(k * 1024)
    for h in range(2):
        mine = row_energy[:, h * 512 : (h + 1) * 512]
        er_ref[h] = jnp.broadcast_to(mine, (128, 512)).T
        ec_ref[h] = col_energy[:, h * 512 : (h + 1) * 512]
    pl.semaphore_wait(barrier, 15)

    used = [0, 0]
    pending = {}

    def send(src, dst, device):
        i = used[0]
        used[0] += 1
        copy = pltpu.make_async_remote_copy(
            src_ref=src, dst_ref=dst, send_sem=ss.at[i], recv_sem=rs.at[i],
            device_id=device, device_id_type=MESH,
        )
        copy.start()
        pending[id(copy)] = copy
        return copy

    def local(src, dst):
        i = used[1]
        used[1] += 1
        copy = pltpu.make_async_copy(src, dst, ls.at[i])
        copy.start()
        return copy

    def sent(copies):
        for copy in copies:
            if pending.pop(id(copy), None) is not None:
                copy.wait_send()

    def all_to_all(ax, src, dst):
        mine = local(src(ax.me), dst(ax.me))
        copies = []
        for d in (4, 3, 5, 2, 6, 1, 7):
            to = rem(ax.me + d, 8)
            copies.append(send(src(to), dst(ax.me), ax.device(to)))

        def wait():
            for copy in copies:
                copy.wait_recv()
            mine.wait()

        return wait

    class Drip:
        def __init__(self, ax, src, dst):
            self.ax, self.src, self.dst = ax, src, dst
            self.mine = local(src(ax.me), dst(ax.me))
            self.left, self.copies = [4, 3, 5, 2, 6, 1, 7], []

        def __call__(self, n):
            for d in self.left[:n]:
                to = rem(self.ax.me + d, 8)
                self.copies.append(send(self.src(to), self.dst(self.ax.me), self.ax.device(to)))
            self.left = self.left[n:]

        def wait(self):
            for copy in self.copies:
                copy.wait_recv()
            self.mine.wait()

    class Scatter:
        def __init__(self, ax, part, far, near, stage, mate_land):
            self.ax, self.part, self.far, self.near = ax, part, far, near
            self.stage, self.mate_land = stage, mate_land
            self.far_copies, self.near_copies = [None, None], [None, None]

        def at(self, d, m):
            mate = (1 - self.ax.mate) if m == 0 else self.ax.mate
            return self.ax.index(rem(self.ax.ring + d, 4), mate)

        def next(self, d):
            return self.ax.device(self.ax.index(rem(self.ax.ring + d, 4), self.ax.mate))

        def start(self, m):
            self.far_copies[m] = [
                send(self.ax.half(self.part, self.at(2, m), h), self.far.at[m, h], self.next((1, 3)[h]))
                for h in range(2)
            ]

        def step(self, m):
            self.near_copies[m] = []
            for h in range(2):
                d = (1, 3)[h]
                self.far_copies[m][h].wait_recv()
                half = self.ax.half(self.part, self.at(d, m), h)
                half[...] = half[...] + self.far[m, h]
                self.near_copies[m].append(
                    send(self.ax.pick(self.part, self.at(d, m)), self.near.at[m, h], self.next(d))
                )

        def total(self, m):
            for copy in self.near_copies[m]:
                copy.wait_recv()
            return self.ax.pick(self.part, self.at(0, m))[...] + (self.near[m, 0] + self.near[m, 1])

        def to_mate(self):
            self.stage[...] = self.total(0)
            self.mate_copy = send(self.stage, self.mate_land, self.ax.device(self.at(0, 0)))

        def end(self):
            value = self.total(1)
            self.mate_copy.wait_recv()
            return value + self.mate_land[...]

        def copies(self):
            return sum(self.far_copies + self.near_copies, []) + [self.mate_copy]

    class Gather:
        def __init__(self, ax, full, also=None):
            self.ax, self.full = ax, full
            self.also = also if also is not None else (lambda i: None)

        def at(self, d, m):
            mate = (1 - self.ax.mate) if m == 0 else self.ax.mate
            return self.ax.index(rem(self.ax.ring + d, 4), mate)

        def both_ways(self, m):
            piece = self.ax.pick(self.full, self.at(0, m))
            self.also(self.at(0, m))
            return [send(piece, piece, self.ax.device(self.at(d, 1))) for d in (1, 3)]

        def onward(self, m, copies):
            out = []
            for h in range(2):
                copies[h].wait_recv()
                i = self.at((3, 1)[h], m)
                piece = self.ax.half(self.full, i, h)
                out.append(send(piece, piece, self.ax.device(self.at((1, 3)[h], 1))))
                self.also(i)
            return out

        def start(self):
            piece = self.ax.pick(self.full, self.ax.me)
            self.mate_copy = send(piece, piece, self.ax.device(self.at(0, 0)))
            self.own = self.both_ways(1)

        def step1(self):
            self.own_far = self.onward(1, self.own)

        def step2(self):
            self.mate_copy.wait_recv()
            self.other = self.both_ways(0)

        def step3(self):
            self.other_far = self.onward(0, self.other)

        def end(self):
            for m, copies in ((1, self.own_far), (0, self.other_far)):
                for copy in copies:
                    copy.wait_recv()
                self.also(self.at(2, m))

    def lanes(n, size):
        return pl.ds(pl.multiple_of(n * size, size), size)

    a_copy = send(a_ref.at[o], a_in, sibling)
    f_copy = send(f_ref, f_sib, sibling)
    f_mine = local(f_ref.at[row], fg.at[k])
    f_mine.wait()
    f_gather = Gather(col_ax, fg)
    f_gather.start()
    v_hop1 = all_to_all(row_ax, lambda i: v_ref.at[:, i], lambda i: b1.at[i])

    fk_hl[0, c], fk_hl[1, c] = split(f_ref[...].reshape(512, 1024))
    lh[0, :, lanes(c, 512)], lh[1, :, lanes(c, 512)] = split(a_ref[c])
    a_copy.wait_recv()
    lh[0, :, lanes(o, 512)], lh[1, :, lanes(o, 512)] = split(a_in[...])
    f_copy.wait_recv()
    fk_hl[0, o], fk_hl[1, o] = split(f_sib[...].reshape(512, 1024))
    f_gather.step1()
    f_gather.step2()

    def chunk(ref, h):
        return ref.at[(slice(None),) * (len(ref.shape) - 1) + (pl.ds(h * 512, 512),)]

    def product_nn(left, right, out, h):
        @pl.loop(0, 2)
        def _(n):
            cols = pl.ds(pl.multiple_of(h * 512 + n * 256, 256), 256)
            res = triple(
                dot_nn, left[0], left[1],
                right[0, :, :, cols].reshape(1024, 256), right[1, :, :, cols].reshape(1024, 256),
            )
            out[:, :, :, cols] = res.reshape(8, 8, 8, 256)

    def scatters(ax, part, far, near, stage, mate_land):
        return [
            Scatter(ax, chunk(part, h), far.at[h], near.at[h], stage.at[h], mate_land.at[h]) for h in range(2)
        ]

    rs0 = scatters(col_ax, pa, far_c, near_c, sum_c, mate_c)
    i_gather = [Gather(col_ax, chunk(inter, h)) for h in range(2)]
    for h in range(2):
        product_nn(lh, fk_hl, pa, h)
        rs0[h].start(0)
        rs0[h].start(1)
    f_gather.step3()
    v_copy = send(v_ref.at[o], v_in, sibling)
    rs0[0].step(0)
    rs0[0].step(1)
    rs0[0].to_mate()
    rs0[1].step(0)
    f_gather.end()

    def start_inter(h):
        chunk(inter, h)[k] = rs0[h].end()
        i_gather[h].start()

    start_inter(0)
    rs0[1].step(1)
    rs0[1].to_mate()
    i_gather[0].step1()
    i_gather[0].step2()
    start_inter(1)
    i_gather[0].step3()
    i_gather[1].step1()
    i_gather[1].step2()
    f_hop = all_to_all(row_ax, lambda i: fg.at[i], lambda i: fr.at[c, i])
    i_gather[0].end()
    lf[0, :, :512], lf[1, :, :512] = split(inter[:, :, :, :512].reshape(512, 512))
    i_gather[1].step3()
    i_gather[1].end()
    lf[0, :, 512:], lf[1, :, 512:] = split(inter[:, :, :, 512:].reshape(512, 512))
    v_hop1()
    v_hop2 = all_to_all(col_ax, lambda i: b1.at[i], lambda i: b2.at[i])

    v_copy.wait_recv()

    @pl.loop(0, 2)
    def _(n):
        rows = lanes(n, 256)
        res = triple(dot_nt, lf[0], lf[1], fk_hl[0, o, rows], fk_hl[1, o, rows])
        drive = v_in[:, :, rows].reshape(512, 256)
        y = (drive + res) / (er_ref[c, :, :1] + ec_ref[o, :, rows])
        y_out[:, rows] = y
        at = pl.ds(pl.multiple_of(o * 512 + n * 256, 256), 256)
        lh[0, :, at], lh[1, :, at] = split(y)

    y_copy = send(y_out, y_in, sibling)

    @pl.loop(0, 2)
    def _(n):
        rows = lanes(n, 256)
        res = triple(dot_nt, lf[0], lf[1], fk_hl[0, c, rows], fk_hl[1, c, rows])
        drive = v_ref[c, :, :, rows].reshape(512, 256)
        y = (drive + res) / (er_ref[c, :, :1] + ec_ref[c, :, rows])
        at = pl.ds(pl.multiple_of(c * 512 + n * 256, 256), 256)
        lh[0, :, at], lh[1, :, at] = split(y)
        lt[0, rows, lanes(c, 512)], lt[1, rows, lanes(c, 512)] = split(y.T)

    f_hop()
    f_copy2 = send(fr.at[c], fr.at[c], sibling)
    sent(rs0[0].copies() + rs0[1].copies())
    rs1_c = scatters(col_ax, pa, far_c, near_c, sum_c, mate_c)
    rs1_r = scatters(row_ax, pb, far_r, near_r, sum_r, mate_r)
    for h in range(2):
        product_nn(lh, fk_hl, pa, h)
        rs1_c[h].start(0)
        rs1_c[h].start(1)
    y_copy.wait_recv()

    @pl.loop(0, 2)
    def _(n):
        rows = lanes(n, 256)
        lt[0, rows, lanes(o, 512)], lt[1, rows, lanes(o, 512)] = split(y_in[:, rows].T)

    fr_hl[0, c], fr_hl[1, c] = split(fr[c].reshape(512, 1024))
    f_copy2.wait_recv()
    fr_hl[0, o], fr_hl[1, o] = split(fr[o].reshape(512, 1024))
    for h in range(2):
        product_nn(lt, fr_hl, pb, h)
        rs1_r[h].start(0)
        rs1_r[h].start(1)
        if h == 0:
            rs1_c[0].step(0)
            rs1_c[0].step(1)

    c_hop1, r_hop1, c_hop2, r_hop2 = [None] * 2, [None] * 2, [None] * 2, [None] * 2
    k_gather = [Gather(row_ax, chunk(wk, h)) for h in range(2)]
    r_gather = [Gather(col_ax, chunk(wr.at[c], h)) for h in range(2)]

    def end_c(h):
        own_c[h] = (2.0 * KEEP * OMEGA) * chunk(inter, h)[k] - (OMEGA * OMEGA) * rs1_c[h].end()
        c_hop1[h] = all_to_all(row_ax, lambda i: own_c.at[h, i], lambda i: t1.at[h, i])

    def end_r(h):
        own_r[h] = -(OMEGA * OMEGA) * rs1_r[h].end()
        r_hop1[h] = all_to_all(col_ax, lambda i: own_r.at[h, i], lambda i: u1.at[h, i])

    def second_hops(h):
        c_hop1[h]()
        c_hop2[h] = all_to_all(col_ax, lambda i: t1.at[h, i], lambda i: t2.at[h, i])
        r_hop1[h]()
        r_hop2[h] = all_to_all(row_ax, lambda i: u1.at[h, i], lambda i: u2.at[h, i])

    def start_gathers(h):
        c_hop2[h]()
        row_ax.pick(chunk(wk, h), row)[...] = own_r[h] + t2[h]
        k_gather[h].start()
        r_hop2[h]()
        col_ax.pick(chunk(wr.at[c], h), k)[...] = own_c[h] + u2[h]
        r_gather[h].start()

    rs1_c[0].to_mate()
    rs1_c[1].step(0)
    rs1_r[0].step(0)
    rs1_r[0].step(1)
    end_c(0)
    rs1_c[1].step(1)
    rs1_r[0].to_mate()
    rs1_r[1].step(0)
    rs1_c[1].to_mate()
    end_r(0)
    rs1_r[1].step(1)
    end_c(1)
    rs1_r[1].to_mate()
    second_hops(0)
    end_r(1)
    start_gathers(0)
    v_hop2()
    v_hop3 = Drip(row_ax, lambda i: b2.at[i], lambda i: b3.at[i])
    v_hop3(2)
    second_hops(1)
    for gather in (k_gather[0], r_gather[0]):
        gather.step1()
        gather.step2()
    start_gathers(1)
    v_hop3(1)
    v_hop3(2)
    k_gather[0].step3()
    r_gather[0].step3()
    v_hop3(2)
    for gather in (k_gather[1], r_gather[1]):
        gather.step1()
        gather.step2()

    def take(h):
        cols = pl.ds(h * 512, 512)
        copy = send(chunk(wr.at[c], h), chunk(wr.at[c], h), sibling)
        lf[0, :, cols], lf[1, :, cols] = split(wr[c, :, :, :, cols].reshape(512, 512))
        lt[0, :, cols], lt[1, :, cols] = split(wk[:, :, :, cols].reshape(512, 512))
        return copy

    def take_sibling(h, copy):
        cols = pl.ds(h * 512, 512)
        copy.wait_recv()
        lh[0, :, cols], lh[1, :, cols] = split(wr[o, :, :, :, cols].reshape(512, 512))

    def terms(half, left, n, h):
        rows, cols = lanes(n, 256), pl.ds(h * 512, 512)
        return triple(
            dot_nt, left[0, :, cols], left[1, :, cols], fk_hl[0, c, rows, cols], fk_hl[1, c, rows, cols]
        ) + triple(
            dot_nt, fr_hl[0, half, :, cols], fr_hl[1, half, :, cols], lt[0, rows, cols], lt[1, rows, cols]
        )

    def first(half, left):
        @pl.loop(0, 2)
        def _(n):
            o_ref[half, :, lanes(n, 256)] = terms(half, left, n, 0)

    k_gather[0].end()
    r_gather[0].end()
    w_copy = take(0)
    k_gather[1].step3()
    r_gather[1].step3()
    first(c, lf)
    take_sibling(0, w_copy)
    first(o, lh)
    k_gather[1].end()
    r_gather[1].end()
    w_copy = take(1)
    v_hop3.wait()
    vt_copy = send(b3.at[:, o], vt_sib, sibling)

    def finish(half, left, mirrored):
        @pl.loop(0, 2)
        def _(n):
            rows = lanes(n, 256)
            res = o_ref[half, :, rows] + terms(half, left, n, 1)
            drive = v_ref[half, :, :, rows].reshape(512, 256) + mirrored(n).reshape(256, 512).T
            sym = (1.0 + KEEP) * OMEGA * drive + res
            o_ref[half, :, rows] = (KEEP * KEEP) * a_ref[half, :, rows] - sym / (
                er_ref[half, :, :1] + ec_ref[c, :, rows]
            )

    finish(c, lf, lambda n: b3[pl.ds(n * 4, 4), c])
    take_sibling(1, w_copy)
    vt_copy.wait_recv()
    finish(o, lh, lambda n: vt_sib[pl.ds(n * 4, 4)])
    sent(list(pending.values()))


def on_device(amplitudes, integrals, factors, pair_order, occ_energy, vir_energy):
    big = lambda *shape: pltpu.VMEM(shape, F32)
    half = lambda *shape: pltpu.VMEM(shape, BF16)
    out = pl.pallas_call(
        kernel,
        out_shape=jax.ShapeDtypeStruct((2, 512, 512), F32),
        in_specs=[pl.BlockSpec(memory_space=pltpu.VMEM)] * 6,
        out_specs=pl.BlockSpec(memory_space=pltpu.VMEM),
        scratch_shapes=[
            big(512, 512),
            big(8, 64, 512),
            big(8, 8, 8, 1024),
            half(2, 2, 512, 1024),
            big(2, 8, 8, 8, 1024),
            half(2, 2, 512, 1024),
            big(8, 8, 8, 1024),
            big(2, 2, 2, 4, 8, 512),
            big(2, 2, 2, 8, 8, 512),
            big(2, 2, 2, 4, 8, 512),
            big(2, 2, 2, 8, 8, 512),
            big(2, 8, 8, 512),
            big(2, 8, 8, 512),
            big(2, 8, 8, 512),
            big(2, 8, 8, 512),
            big(2, 8, 8, 512),
            big(2, 8, 8, 512),
            big(8, 8, 8, 1024),
            big(512, 512),
            half(2, 512, 1024),
            half(2, 512, 1024),
            half(2, 512, 1024),
            big(2, 8, 8, 8, 1024),
            big(8, 8, 8, 1024),
            big(8, 2, 64, 512),
            big(8, 2, 64, 512),
            big(8, 2, 64, 512),
            big(8, 64, 512),
            big(2, 8, 8, 512),
            big(2, 8, 8, 512),
            big(2, 8, 8, 512),
            big(2, 8, 8, 512),
            big(8, 8, 8, 1024),
            big(2, 512, 128),
            big(2, 1, 512),
            pltpu.SemaphoreType.DMA((N_SEM,)),
            pltpu.SemaphoreType.DMA((N_SEM,)),
            pltpu.SemaphoreType.DMA((16,)),
        ],
        compiler_params=pltpu.CompilerParams(
            collective_id=0, has_side_effects=True, vmem_limit_bytes=63 * 2**20
        ),
        name="lambda_steps",
    )(
        amplitudes.reshape(2, 512, 512),
        integrals.reshape(2, 8, 64, 512),
        factors.reshape(8, 8, 8, 1024),
        pair_order.reshape(1, NO * NV),
        occ_energy.reshape(1, NO),
        vir_energy.reshape(1, NV),
    )
    return out.reshape(1024, 512)


def solution(mesh):
    return jax.shard_map(
        on_device,
        mesh=mesh,
        in_specs=(P("row", "col"), P("row", "col"), P("col", None), P(), P(), P()),
        out_specs=P("row", "col"),
        check_vma=False,
    )
```
